32 devices in a mesh: groups: 2 (over y), dp: 4 (over z), tensor: 4 (over x, core).
Axes of the slice: x: 2, y: 2, z: 4, core: 2. Of those that a mesh axis runs over, the one named last changes fastest.
Arguments:
- activations: bfloat16 [16, 128, 28672], P(('groups', 'dp'), None, 'tensor'), parts along dimension 0, may hold values from -6 to 6
- out_grads: bfloat16 [16, 128, 8192], P(('groups', 'dp'), None, 'tensor'), parts along dimension 0, may hold values from -6 to 6
- proj_in: bfloat16 [28672, 64], P('tensor'), may hold values from -0.03125 to 0.03125
- proj_out: bfloat16 [8192, 64], P('tensor'), may hold values from -0.0625 to 0.0625
- lengths: int32 [16], P(('groups', 'dp')), parts along dimension 0, may hold values from 64 to 128, as said below
- query_ids: int32 [128], P('groups'), parts along dimension 0, may hold values from 0 to 7
Outputs:
- scores: float32 [64, 16], P(None, ('groups', 'dp')), parts along dimension 1
The draws below stay inside these ranges and needn't reach their ends.
There are 2 independent parts, one for each index of `groups`. The reference program is written for one: setup_inputs(seed, part) draws one part's arguments, and reference() takes and returns one part's arrays. A program takes and returns all parts, laid end to end along the dimension named above; an argument that names none is the same for every part. Nothing has to cross between parts.
Inputs may be any that keep to these rules, and one draw needn't show every extreme that they name: `lengths`: some example has exactly 128 live tokens.
All inputs are finite; a program needn't handle non-finite values.
Results may differ from the reference program's by a relative error of at most 0.0003.
Values sent between devices are 32-bit elements; how exact they have to be, the bound alone decides.
No kernel may reach another device: no remote copies, remote signals or barrier semaphores. Data moves between devices by JAX's collectives and lax.ppermute only.
A program may use at most 64 MiB of HBM per device.

```python
import jax
import jax.numpy as jnp
from jax import lax

D = 8192
FF = 28672
R = 64
L = 128
QUERIES = 64
EXAMPLES = 8


def draw_lengths(key, part):
    key = jax.random.fold_in(key, 11)
    first, second = jax.random.split(key)
    drawn = jax.random.randint(first, (EXAMPLES,), L // 2, L + 1)
    chosen = jax.random.randint(second, (), 0, EXAMPLES)
    return jnp.where(jnp.arange(EXAMPLES) == chosen, L, drawn).astype(jnp.int32)


def set_ends(values, key, smallest, largest):
    index_at = [jax.random.randint(jax.random.fold_in(key, axis), (), 0, length) for axis, length in enumerate(values.shape)]
    main_axis = values.shape.index(max(values.shape))
    neighbour = index_at[:main_axis] + [(index_at[main_axis] + 1) % values.shape[main_axis]] + index_at[main_axis + 1:]
    return values.at[tuple(index_at)].set(smallest).at[tuple(neighbour)].set(largest)


def level_of(own_key, dims, shards, least, top_value):
    loudness, own = 1.0, jax.random.fold_in(own_key, 6)
    for dim, parts in shards:
        heights = jnp.exp(jax.random.uniform(jax.random.fold_in(own, dim), (parts,), jnp.float32, least / len(shards), top_value / len(shards)))
        loudness = loudness * jnp.repeat(heights, dims[dim] // parts).reshape([-1 if axis == dim else 1 for axis in range(len(dims))])
    return loudness


def centred(key, extent, width, limit, shards=(), held_as=jnp.bfloat16):
    loudness = level_of(key, extent, shards, -0.22, 0.18) if shards else 1.0
    result = jax.random.normal(key, extent, jnp.float32) * width * loudness
    return jnp.minimum(jnp.maximum(result, -limit), limit).astype(held_as)


def setup_inputs(seed: int = 0, part: int = 0) -> dict:
    key_list = jax.random.split(jax.random.key(seed), 7)
    part_splits = jax.random.split(jax.random.fold_in(key_list[6], part), 7)
    activations = centred(part_splits[0], (EXAMPLES, L, FF), 1.0, 6.0, ((0, 4), (2, 4)))
    out_grads = centred(part_splits[1], (EXAMPLES, L, D), 1.0, 6.0, ((0, 4), (2, 4)))
    proj_in = centred(key_list[2], (FF, R), FF ** -0.5, 0.03125, ((0, 4),))
    proj_out = centred(key_list[3], (D, R), D ** -0.5, 0.0625, ((0, 4),))
    lengths = draw_lengths(jax.random.fold_in(jax.random.fold_in(key_list[6], part), 71), part)
    query_ids = set_ends(jax.random.randint(part_splits[5], (QUERIES,), 0, EXAMPLES), jax.random.fold_in(part_splits[5], 1), 0, EXAMPLES - 1).astype(jnp.int32)
    return {"activations": activations, "out_grads": out_grads, "proj_in": proj_in, "proj_out": proj_out, "lengths": lengths, "query_ids": query_ids}


def damped_inverse(cov):
    eye_mat = jnp.eye(R, dtype=jnp.float32)
    damped = cov + 0.1 * jnp.trace(cov) / R * eye_mat
    factor = jnp.linalg.cholesky(damped)
    return jax.scipy.linalg.cho_solve((factor, True), eye_mat)

def reference(activations, out_grads, proj_in, proj_out, lengths, query_ids):
    in_sk = jnp.dot(activations.reshape(-1, FF).astype(jnp.float32), proj_in.astype(jnp.float32), preferred_element_type=jnp.float32).reshape(EXAMPLES, L, R)
    out_sk = jnp.dot(out_grads.reshape(-1, D).astype(jnp.float32), proj_out.astype(jnp.float32), preferred_element_type=jnp.float32).reshape(EXAMPLES, L, R)
    live_mask = jnp.arange(L, dtype=jnp.int32)[None, :] < lengths[:, None]
    in_sk = jnp.where(live_mask[:, :, None], in_sk, 0.0)
    out_sk = jnp.where(live_mask[:, :, None], out_sk, 0.0)
    count = jnp.sum(lengths).astype(jnp.float32)
    high = lax.Precision.HIGHEST
    cov_in = jnp.einsum('elr,els->rs', in_sk, in_sk, precision=high) / count
    cov_out = jnp.einsum('elr,els->rs', out_sk, out_sk, precision=high) / count
    inv_in = damped_inverse(cov_in)
    inv_out = damped_inverse(cov_out)
    sketch = jnp.einsum('ela,elb->eab', out_sk, in_sk, precision=high)
    query = sketch[query_ids]
    conditioned = jnp.einsum('ab,jbc,cd->jad', inv_out, query, inv_in, precision=high)
    return jnp.einsum('jab,eab->je', conditioned, sketch, precision=high) / (R * L)
```

```python
import functools

import jax
import jax.numpy as jnp
from jax import lax
from jax.experimental import pallas as pl
from jax.experimental.pallas import tpu as pltpu
from jax.sharding import PartitionSpec as P

HIGH = lax.Precision.HIGHEST
VMEM = pl.BlockSpec(memory_space=pltpu.VMEM)
SMEM = pl.BlockSpec(memory_space=pltpu.SMEM)
ANY = pl.BlockSpec(memory_space=pl.ANY)
DAMP = 0.1


def dot_nt(a, b):
    return lax.dot_general(a, b, (((1,), (1,)), ((), ())), preferred_element_type=jnp.float32)


def dot_hi(a, b):
    return jnp.dot(a, b, precision=HIGH, preferred_element_type=jnp.float32)


def project_kernel(place, lengths, act, grad, proj_in, proj_out, keep, send, act_v, grad_v, pin_v, pout_v, sems):
    chunks = sems.shape[0] - 1
    width = act.shape[2] // chunks
    copies = []

    def begin(src, dst, slot):
        copy = pltpu.make_async_copy(src, dst, sems.at[slot, len(copies) % 2])
        copy.start()
        copies.append(copy)

    begin(proj_out, pout_v, 0)
    begin(grad, grad_v, 0)
    for n in range(chunks):
        span = pl.ds(n * width, width)
        begin(proj_in.at[:, span], pin_v.at[:, span], n + 1)
        begin(act.at[:, :, span], act_v.at[:, :, span], n + 1)
    examples, seq_len, _ = act.shape
    rank = proj_in.shape[0]
    copies[0].wait()
    copies[1].wait()
    out_part = dot_nt(grad_v[...].reshape(examples * seq_len, -1), pout_v[...])
    in_part = jnp.zeros((examples * seq_len, rank), jnp.float32)
    for n in range(chunks):
        copies[2 * n + 2].wait()
        copies[2 * n + 3].wait()
        span = pl.ds(n * width, width)
        in_part += dot_nt(act_v[:, :, span].reshape(examples * seq_len, width), pin_v[:, span])
    both = jnp.concatenate([out_part, in_part], axis=1)
    token = lax.broadcasted_iota(jnp.int32, (seq_len, 2 * rank), 0)
    first = jnp.where(token < lengths[0], both[:seq_len], 0.0)
    second = jnp.where(token < lengths[1], both[seq_len:], 0.0)
    own = place[0] == 0
    keep[...] = jnp.where(own, first, second)
    send[...] = jnp.where(own, second, first)


def gram_kernel(place, lengths, mine, theirs, packed):
    tokens = mine[...] + theirs[...]
    rank = tokens.shape[1] // 2
    gram = lax.dot_general(
        tokens, tokens, (((0,), (0,)), ((), ())), precision=HIGH, preferred_element_type=jnp.float32
    )
    top = pltpu.roll(gram[:rank], rank, 1)
    low = gram[rank:]
    row = lax.broadcasted_iota(jnp.int32, (rank, 2 * rank), 0)
    lane = lax.broadcasted_iota(jnp.int32, (rank, 2 * rank), 1)
    packed[:rank] = jnp.where(lane <= rank + row, top, low)
    diag = jnp.sum(jnp.where(lane == rank + row, low, 0.0), axis=0, keepdims=True)
    live = lengths[place[0]].astype(jnp.float32)
    tail = jnp.broadcast_to(diag, (8, 2 * rank))
    packed[rank:] = jnp.where(lax.broadcasted_iota(jnp.int32, (8, 2 * rank), 1) < rank, live, tail)


def collect_kernel(*refs):
    packs, total, sketches = refs[:-2], refs[-2], refs[-1]
    rank = packs[0].shape[1] // 2
    parts = [ref[...] for ref in packs]
    lane = lax.broadcasted_iota(jnp.int32, (rank, 2 * rank), 1)
    for n in range(len(parts) // 2):
        sketches[n] = jnp.where(lane < rank, parts[2 * n][:rank], pltpu.roll(parts[2 * n + 1][:rank], rank, 1))
    while len(parts) > 1:
        parts = [parts[n] + parts[n + 1] for n in range(0, len(parts), 2)]
    total[...] = parts[0]


def inverse_steps(rank):
    least = 2.0 * (DAMP / rank) / (1.0 + 2.0 * DAMP / rank)
    scales = []
    while (1.0 - least) ** 2 > 1e-7:
        image = least * (2.0 - least)
        scales.append(2.0 / (1.0 + image))
        least = scales[-1] * image
    return scales + [1.0]


def inverse_kernel(mine, theirs, inv_out, inv_in, scale_out, scale_in):
    total = mine[...] + theirs[...]
    rank = total.shape[1] // 2
    mixed = total[:rank, rank:]
    turned = mixed.T
    diag = total[rank : rank + 1, rank:]
    count = total[rank : rank + 1, :1]
    row = lax.broadcasted_iota(jnp.int32, (rank, rank), 0)
    lane = lax.broadcasted_iota(jnp.int32, (rank, rank), 1)
    eye = row == lane
    sum_out = jnp.where(lane <= row, mixed, turned)
    sum_in = jnp.where(lane > row, mixed, jnp.where(eye, diag, turned))
    factor = 2.0 / (1.0 + 2.0 * DAMP / rank)

    def start(sums):
        trace = jnp.sum(jnp.sum(jnp.where(eye, sums, 0.0), axis=0, keepdims=True), axis=1, keepdims=True)
        return sums * (factor / trace) + jnp.where(eye, factor * DAMP / rank, 0.0), factor * count / trace

    t_out, c_out = start(sum_out)
    t_in, c_in = start(sum_in)
    steps = inverse_steps(rank)
    two_eye = jnp.where(eye, 2.0, 0.0)
    x_out = steps[0] * (two_eye - t_out)
    x_in = steps[0] * (two_eye - t_in)
    t_out = steps[0] * (2.0 * t_out - dot_hi(t_out, t_out))
    t_in = steps[0] * (2.0 * t_in - dot_hi(t_in, t_in))
    for n, scale in enumerate(steps[1:]):
        x_out, x_in, p_out, p_in = (
            scale * (2.0 * x_out - dot_hi(x_out, t_out)),
            scale * (2.0 * x_in - dot_hi(x_in, t_in)),
            t_out,
            t_in,
        )
        if n < len(steps) - 2:
            t_out = scale * (2.0 * p_out - dot_hi(p_out, p_out))
            t_in = scale * (2.0 * p_in - dot_hi(p_in, p_in))
    inv_out[...] = x_out
    inv_in[...] = x_in
    scale_out[...] = jnp.broadcast_to(c_out, scale_out.shape)
    scale_in[...] = jnp.broadcast_to(c_in, scale_in.shape)


def score_kernel(place, queries, mine, theirs, inv_out, inv_in, scale_out, scale_in, scores):
    pairs = mine.shape[0]
    rank = mine.shape[1]
    right = jnp.concatenate([inv_in[...], inv_in[...]], axis=1)
    left = inv_out[...]
    blocks = [mine[n] for n in range(pairs)] + [theirs[n] for n in range(pairs)]
    rows = []
    for own in (mine[0][:, :rank], theirs[0][:, :rank]):
        half = dot_hi(left, own) * scale_out[:1, :1]
        whole = dot_hi(half, right) * scale_in[:1, :1]
        for block in blocks:
            rows.append(jnp.sum(block * whole, axis=0, keepdims=True))
    sums = jnp.concatenate(rows, axis=0)
    height = len(rows)
    num = queries.shape[1]
    index = lax.broadcasted_iota(jnp.int32, (height, num), 0) % (2 * pairs)
    core = place[0] ^ (index // pairs)
    chosen = queries[...]
    terms = jnp.zeros((height, num), jnp.float32)
    for half in range(2):
        value = jnp.sum(sums[:, half * rank : (half + 1) * rank], axis=1, keepdims=True)
        example = (place[1] ^ (2 * (index % pairs) + half)) * 2 + core
        terms += jnp.where(chosen == example, value, 0.0)
    terms = terms * (1.0 / place[2].astype(jnp.float32))
    here = jnp.sum(terms[: height // 2], axis=0, keepdims=True)
    there = jnp.sum(terms[height // 2 :], axis=0, keepdims=True)
    own = place[0] == 0
    scores[0:1, :] = jnp.where(own, here, there)
    scores[1:2, :] = jnp.where(own, there, here)


def shape(*dims):
    return jax.ShapeDtypeStruct(dims, jnp.float32)


def mirror(size, step):
    return [(n, n ^ step) for n in range(size)]


def per_device(dp, tensor, activations, out_grads, proj_in, proj_out, lengths, query_ids):
    examples, seq_len, hidden = activations.shape
    rank = proj_in.shape[1]
    num = query_ids.shape[0]
    chunks = 7 if hidden % (7 * 128) == 0 else 1
    side = lax.axis_index("tensor") % 2
    depth = lax.axis_index("dp")
    place = jnp.stack([side, depth, jnp.int32(rank * seq_len)]).astype(jnp.int32)
    pin_t, pout_t = proj_in.T, proj_out.T
    keep, send = pl.pallas_call(
        project_kernel,
        out_shape=[shape(seq_len, 2 * rank)] * 2,
        in_specs=[SMEM, SMEM, ANY, ANY, ANY, ANY],
        out_specs=[VMEM, VMEM],
        scratch_shapes=[
            pltpu.VMEM(activations.shape, jnp.bfloat16),
            pltpu.VMEM(out_grads.shape, jnp.bfloat16),
            pltpu.VMEM(pin_t.shape, jnp.bfloat16),
            pltpu.VMEM(pout_t.shape, jnp.bfloat16),
            pltpu.SemaphoreType.DMA((chunks + 1, 2)),
        ],
        compiler_params=pltpu.CompilerParams(vmem_limit_bytes=24 * 2**20),
        name="project",
    )(place, lengths, activations, out_grads, pin_t, pout_t)
    total = keep + lax.ppermute(send, "tensor", mirror(tensor, 1))
    step = 2
    while 2 * step < tensor:
        total = total + lax.ppermute(total, "tensor", mirror(tensor, step))
        step *= 2
    other = lax.ppermute(total, "tensor", mirror(tensor, step)) if step < tensor else jnp.zeros_like(total)
    packed = pl.pallas_call(
        gram_kernel,
        out_shape=shape(rank + 8, 2 * rank),
        in_specs=[SMEM, SMEM, VMEM, VMEM],
        out_specs=VMEM,
        name="gram",
    )(place, lengths, total, other)
    if dp <= 4:
        packs = [packed] + [lax.ppermute(packed, "dp", mirror(dp, step)) for step in range(1, dp)]
    else:
        gathered = lax.all_gather(packed, "dp", axis=0)[depth ^ jnp.arange(dp, dtype=jnp.int32)]
        packs = [gathered[n] for n in range(dp)]
    summed, sketches = pl.pallas_call(
        collect_kernel,
        out_shape=[shape(rank + 8, 2 * rank), shape(dp // 2, rank, 2 * rank)],
        in_specs=[VMEM] * dp,
        out_specs=[VMEM, VMEM],
        name="collect",
    )(*packs)
    summed_other = lax.ppermute(summed, "tensor", mirror(tensor, 1))
    sketches_other = lax.ppermute(sketches, "tensor", mirror(tensor, 1))
    inverses = pl.pallas_call(
        inverse_kernel,
        out_shape=[shape(rank, rank), shape(rank, rank), shape(8, 128), shape(8, 128)],
        in_specs=[VMEM, VMEM],
        out_specs=[VMEM] * 4,
        name="inverse",
    )(summed, summed_other)
    scores = pl.pallas_call(
        score_kernel,
        out_shape=shape(examples, num),
        in_specs=[SMEM] + [VMEM] * 7,
        out_specs=VMEM,
        name="scores",
    )(place, query_ids.reshape(1, num), sketches, sketches_other, *inverses)
    return scores.T


def solution(mesh):
    placed = (
        P(("groups", "dp"), None, "tensor"),
        P(("groups", "dp"), None, "tensor"),
        P("tensor", None),
        P("tensor", None),
        P(("groups", "dp")),
        P("groups"),
    )
    return jax.shard_map(
        functools.partial(per_device, mesh.shape["dp"], mesh.shape["tensor"]),
        mesh=mesh,
        in_specs=placed,
        out_specs=P(None, ("groups", "dp")),
        check_vma=False,
    )
```

```python
import functools

import jax
import jax.numpy as jnp
from jax import lax
from jax.experimental import pallas as pl
from jax.experimental.pallas import tpu as pltpu
from jax.sharding import PartitionSpec as P

HIGH = lax.Precision.HIGHEST
VMEM = pl.BlockSpec(memory_space=pltpu.VMEM)
HBM = pl.BlockSpec(memory_space=pltpu.HBM)
DAMP = 0.1


def dot_nt(a, b):
    return lax.dot_general(a, b, (((1,), (1,)), ((), ())), preferred_element_type=jnp.float32)


def dot_hi(a, b):
    return jnp.dot(a, b, precision=HIGH, preferred_element_type=jnp.float32)


def project_kernel(lengths, act, grad, proj_in, proj_out, keep, send, live, len_s, act_v, grad_v, pin_v, pout_v, sems):
    chunks = sems.shape[0] - 2
    width = act.shape[2] // chunks
    copies = []

    def begin(src, dst, slot):
        copy = pltpu.make_async_copy(src, dst, sems.at[slot, len(copies) % 2])
        copy.start()
        copies.append(copy)

    begin(proj_out, pout_v, 0)
    begin(grad, grad_v, 0)
    begin(lengths, len_s, chunks + 1)
    for n in range(chunks):
        span = pl.ds(n * width, width)
        begin(proj_in.at[:, span], pin_v.at[:, span], n + 1)
        begin(act.at[:, :, span], act_v.at[:, :, span], n + 1)
    examples, seq_len, _ = act.shape
    rank = proj_in.shape[0]
    copies[0].wait()
    copies[1].wait()
    out_part = dot_nt(grad_v[...].reshape(examples * seq_len, -1), pout_v[...])
    in_part = jnp.zeros((examples * seq_len, rank), jnp.float32)
    for n in range(chunks):
        copies[2 * n + 3].wait()
        copies[2 * n + 4].wait()
        span = pl.ds(n * width, width)
        in_part += dot_nt(act_v[:, :, span].reshape(examples * seq_len, width), pin_v[:, span])
    both = jnp.concatenate([out_part, in_part], axis=1)
    token = lax.broadcasted_iota(jnp.int32, (seq_len, 2 * rank), 0)
    copies[2].wait()
    first = jnp.where(token < len_s[0], both[:seq_len], 0.0)
    second = jnp.where(token < len_s[1], both[seq_len:], 0.0)
    side = lax.rem(lax.axis_index("tensor"), 2)
    keep[...] = jnp.where(side == 0, first, second)
    send[...] = jnp.where(side == 0, second, first)
    live[...] = jnp.full(live.shape, len_s[side].astype(jnp.float32))


def gram_kernel(live, mine, theirs, packed):
    tokens = mine[...] + theirs[...]
    rank = tokens.shape[1] // 2
    gram = lax.dot_general(
        tokens, tokens, (((0,), (0,)), ((), ())), precision=HIGH, preferred_element_type=jnp.float32
    )
    top = pltpu.roll(gram[:rank], rank, 1)
    low = gram[rank:]
    row = lax.broadcasted_iota(jnp.int32, (rank, 2 * rank), 0)
    lane = lax.broadcasted_iota(jnp.int32, (rank, 2 * rank), 1)
    packed[:rank] = jnp.where(lane <= rank + row, top, low)
    diag = jnp.sum(jnp.where(lane == rank + row, low, 0.0), axis=0, keepdims=True)
    packed[rank:] = jnp.where(lax.broadcasted_iota(jnp.int32, (8, 2 * rank), 1) < rank, live[...], diag)


def collect_kernel(*refs):
    packs, total, sketches = refs[:-2], refs[-2], refs[-1]
    rank = packs[0].shape[1] // 2
    parts = [ref[...] for ref in packs]
    lane = lax.broadcasted_iota(jnp.int32, (rank, 2 * rank), 1)
    for n in range(len(parts) // 2):
        sketches[n] = jnp.where(lane < rank, parts[2 * n][:rank], pltpu.roll(parts[2 * n + 1][:rank], rank, 1))
    while len(parts) > 1:
        parts = [parts[n] + parts[n + 1] for n in range(0, len(parts), 2)]
    total[...] = parts[0]


def inverse_steps(rank):
    least = 2.0 * (DAMP / rank) / (1.0 + 2.0 * DAMP / rank)
    scales = []
    while (1.0 - least) ** 2 > 1e-7:
        image = least * (2.0 - least)
        scales.append(2.0 / (1.0 + image))
        least = scales[-1] * image
    return scales + [1.0]


def inverse_kernel(mine, theirs, inv_out, inv_in, scale_out, scale_in):
    total = mine[...] + theirs[...]
    rank = total.shape[1] // 2
    mixed = total[:rank, rank:]
    turned = mixed.T
    diag = total[rank : rank + 1, rank:]
    count = total[rank : rank + 1, :1]
    row = lax.broadcasted_iota(jnp.int32, (rank, rank), 0)
    lane = lax.broadcasted_iota(jnp.int32, (rank, rank), 1)
    eye = row == lane
    sum_out = jnp.where(lane <= row, mixed, turned)
    sum_in = jnp.where(lane > row, mixed, jnp.where(eye, diag, turned))
    factor = 2.0 / (1.0 + 2.0 * DAMP / rank)

    def start(sums):
        trace = jnp.sum(jnp.sum(jnp.where(eye, sums, 0.0), axis=0, keepdims=True), axis=1, keepdims=True)
        return sums * (factor / trace) + jnp.where(eye, factor * DAMP / rank, 0.0), factor * count / trace

    t_out, c_out = start(sum_out)
    t_in, c_in = start(sum_in)
    steps = inverse_steps(rank)
    two_eye = jnp.where(eye, 2.0, 0.0)
    x_out = steps[0] * (two_eye - t_out)
    x_in = steps[0] * (two_eye - t_in)
    t_out = steps[0] * (2.0 * t_out - dot_hi(t_out, t_out))
    t_in = steps[0] * (2.0 * t_in - dot_hi(t_in, t_in))
    for n, scale in enumerate(steps[1:]):
        x_out, x_in, p_out, p_in = (
            scale * (2.0 * x_out - dot_hi(x_out, t_out)),
            scale * (2.0 * x_in - dot_hi(x_in, t_in)),
            t_out,
            t_in,
        )
        if n < len(steps) - 2:
            t_out = scale * (2.0 * p_out - dot_hi(p_out, p_out))
            t_in = scale * (2.0 * p_in - dot_hi(p_in, p_in))
    inv_out[...] = x_out
    inv_in[...] = x_in
    scale_out[...] = jnp.broadcast_to(c_out, scale_out.shape)
    scale_in[...] = jnp.broadcast_to(c_in, scale_in.shape)


def score_kernel(seq_len, queries, mine, theirs, inv_out, inv_in, scale_out, scale_in, scores):
    pairs = mine.shape[0]
    rank = mine.shape[1]
    right = jnp.concatenate([inv_in[...], inv_in[...]], axis=1)
    left = inv_out[...]
    blocks = [mine[n] for n in range(pairs)] + [theirs[n] for n in range(pairs)]
    rows = []
    for own in (mine[0][:, :rank], theirs[0][:, :rank]):
        half = dot_hi(left, own) * scale_out[:1, :1]
        whole = dot_hi(half, right) * scale_in[:1, :1]
        for block in blocks:
            rows.append(jnp.sum(block * whole, axis=0, keepdims=True))
    sums = jnp.concatenate(rows, axis=0)
    height = len(rows)
    num = queries.shape[1]
    index = lax.broadcasted_iota(jnp.int32, (height, num), 0) % (2 * pairs)
    side = lax.rem(lax.axis_index("tensor"), 2)
    depth = lax.axis_index("dp")
    core = side ^ (index // pairs)
    chosen = queries[...]
    terms = jnp.zeros((height, num), jnp.float32)
    for half in range(2):
        value = jnp.sum(sums[:, half * rank : (half + 1) * rank], axis=1, keepdims=True)
        example = (depth ^ (2 * (index % pairs) + half)) * 2 + core
        terms += jnp.where(chosen == example, value, 0.0)
    terms = terms * (1.0 / (rank * seq_len))
    here = jnp.sum(terms[: height // 2], axis=0, keepdims=True)
    there = jnp.sum(terms[height // 2 :], axis=0, keepdims=True)
    scores[0:1, :] = jnp.where(side == 0, here, there)
    scores[1:2, :] = jnp.where(side == 0, there, here)


def shape(*dims):
    return pltpu.VMEM(dims, jnp.float32)


def call(kernel, name, out_shape, *operands):
    many = isinstance(out_shape, list)
    return pl.pallas_call(
        kernel,
        out_shape=out_shape,
        in_specs=[VMEM] * len(operands),
        out_specs=[VMEM] * len(out_shape) if many else VMEM,
        compiler_params=pltpu.CompilerParams(vmem_limit_bytes=4 * 2**20),
        name=name,
    )(*[pltpu.with_memory_space_constraint(operand, pltpu.VMEM) for operand in operands])


def mirror(size, step):
    return [(n, n ^ step) for n in range(size)]


def project(activations, out_grads, proj_in, proj_out, lengths):
    seq_len, hidden = activations.shape[1:]
    chunks = 7 if hidden % (7 * 128) == 0 else 1
    block = shape(seq_len, 2 * proj_in.shape[0])
    operands = [lengths, activations, out_grads, proj_in, proj_out]
    return pl.pallas_call(
        project_kernel,
        out_shape=[block, block, shape(8, 2 * proj_in.shape[0])],
        in_specs=[HBM] * 5,
        out_specs=[VMEM] * 3,
        scratch_shapes=[pltpu.SMEM(lengths.shape, jnp.int32)]
        + [pltpu.VMEM(operand.shape, jnp.bfloat16) for operand in operands[1:]]
        + [pltpu.SemaphoreType.DMA((chunks + 2, 2))],
        compiler_params=pltpu.CompilerParams(vmem_limit_bytes=24 * 2**20),
        name="project",
    )(*[pltpu.with_memory_space_constraint(operand, pltpu.HBM) for operand in operands])


def per_device(dp, tensor, activations, out_grads, proj_in, proj_out, lengths, query_ids):
    examples, seq_len, _ = activations.shape
    rank = proj_in.shape[1]
    num = query_ids.shape[0]
    keep, send, live = project(activations, out_grads, proj_in.T, proj_out.T, lengths)
    total = keep + lax.ppermute(send, "tensor", mirror(tensor, 1))
    step = 2
    while 2 * step < tensor:
        total = total + lax.ppermute(total, "tensor", mirror(tensor, step))
        step *= 2
    other = lax.ppermute(total, "tensor", mirror(tensor, step)) if step < tensor else jnp.zeros_like(total)
    packed = call(gram_kernel, "gram", shape(rank + 8, 2 * rank), live, total, other)
    if dp <= 4:
        packs = [packed] + [lax.ppermute(packed, "dp", mirror(dp, step)) for step in range(1, dp)]
    else:
        order = lax.axis_index("dp") ^ jnp.arange(dp, dtype=jnp.int32)
        gathered = lax.all_gather(packed, "dp", axis=0)[order]
        packs = [gathered[n] for n in range(dp)]
    results = [shape(rank + 8, 2 * rank), shape(dp // 2, rank, 2 * rank)]
    summed, sketches = call(collect_kernel, "collect", results, *packs)
    summed_other = lax.ppermute(summed, "tensor", mirror(tensor, 1))
    sketches_other = lax.ppermute(sketches, "tensor", mirror(tensor, 1))
    results = [shape(rank, rank), shape(rank, rank), shape(8, 128), shape(8, 128)]
    inverses = call(inverse_kernel, "inverse", results, summed, summed_other)
    scores = call(
        functools.partial(score_kernel, seq_len),
        "scores",
        shape(examples, num),
        query_ids.reshape(1, num),
        sketches,
        sketches_other,
        *inverses,
    )
    return scores.T


def solution(mesh):
    placed = (
        P(("groups", "dp"), None, "tensor"),
        P(("groups", "dp"), None, "tensor"),
        P("tensor", None),
        P("tensor", None),
        P(("groups", "dp")),
        P("groups"),
    )
    return jax.shard_map(
        functools.partial(per_device, mesh.shape["dp"], mesh.shape["tensor"]),
        mesh=mesh,
        in_specs=placed,
        out_specs=P(None, ("groups", "dp")),
        check_vma=False,
    )
```

```python
import functools

import jax
import jax.numpy as jnp
from jax import lax
from jax.experimental import pallas as pl
from jax.experimental.pallas import tpu as pltpu
from jax.sharding import PartitionSpec as P

HIGH = lax.Precision.HIGHEST
VMEM = pl.BlockSpec(memory_space=pltpu.VMEM)
HBM = pl.BlockSpec(memory_space=pltpu.HBM)
DAMP = 0.1


def dot_nt(a, b):
    return lax.dot_general(a, b, (((1,), (1,)), ((), ())), preferred_element_type=jnp.float32)


def dot_hi(a, b):
    return jnp.dot(a, b, precision=HIGH, preferred_element_type=jnp.float32)


def project_kernel(lengths, act, grad, proj_in, proj_out, sketch, live, len_s, act_v, grad_v, pin_v, pout_v, sems):
    chunks = sems.shape[0] - 2
    width = act.shape[2] // chunks
    copies = []

    def begin(src, dst, slot):
        copy = pltpu.make_async_copy(src, dst, sems.at[slot, len(copies) % 2])
        copy.start()
        copies.append(copy)

    begin(proj_out, pout_v, 0)
    begin(grad, grad_v, 0)
    begin(lengths, len_s, chunks + 1)
    for n in range(chunks):
        span = pl.ds(n * width, width)
        begin(proj_in.at[:, span], pin_v.at[:, span], n + 1)
        begin(act.at[:, :, span], act_v.at[:, :, span], n + 1)
    examples, seq_len, _ = act.shape
    rank = proj_in.shape[0]
    copies[0].wait()
    copies[1].wait()
    out_part = dot_nt(grad_v[...].reshape(examples * seq_len, -1), pout_v[...])
    in_part = jnp.zeros((examples * seq_len, rank), jnp.float32)
    for n in range(chunks):
        copies[2 * n + 3].wait()
        copies[2 * n + 4].wait()
        span = pl.ds(n * width, width)
        in_part += dot_nt(act_v[:, :, span].reshape(examples * seq_len, width), pin_v[:, span])
    both = jnp.concatenate([out_part, in_part], axis=1)
    token = lax.broadcasted_iota(jnp.int32, (seq_len, 2 * rank), 0)
    copies[2].wait()
    count = jnp.int32(0)
    for e in range(examples):
        rows = pl.ds(e * seq_len, seq_len)
        sketch[rows] = jnp.where(token < len_s[e], both[e * seq_len : (e + 1) * seq_len], 0.0)
        count += len_s[e]
    live[...] = jnp.full(live.shape, count.astype(jnp.float32))


def gram_kernel(seq_len, leads, live, mine, theirs, packed):
    rank = mine.shape[1] // 2

    @pl.when(leads())
    def _():
        tokens = mine[...] + theirs[...]
        grams = []
        for e in range(2):
            block = tokens[e * seq_len : (e + 1) * seq_len]
            grams.append(
                lax.dot_general(
                    block, block, (((0,), (0,)), ((), ())), precision=HIGH, preferred_element_type=jnp.float32
                )
            )
        total = grams[0] + grams[1]
        low = total[rank:]
        row = lax.broadcasted_iota(jnp.int32, (rank, 2 * rank), 0)
        lane = lax.broadcasted_iota(jnp.int32, (rank, 2 * rank), 1)
        mixed = jnp.where(lane <= row, total[:rank], pltpu.roll(low, rank, 1))
        packed[:rank] = jnp.where(lane < rank, mixed, grams[0][:rank])
        half = rank // 2
        folded = pltpu.roll(grams[1][half:rank], rank, 1)
        packed[rank : rank + half] = jnp.where(lane[:half] < rank, folded, grams[1][:half])
        diag = jnp.sum(jnp.where(lane == rank + row, low, 0.0), axis=0, keepdims=True)
        diag = pltpu.roll(jnp.broadcast_to(diag, (8, 2 * rank)), rank, 1)
        packed[rank + half :] = jnp.where(lane[:8] < rank, diag, live[...])


def unfold(top, folded):
    rank = top.shape[0]
    lane = lax.broadcasted_iota(jnp.int32, top.shape, 1)
    return jnp.where(lane < rank, jnp.concatenate([pltpu.roll(folded, rank, 1), folded], axis=0), top)


def merge_kernel(leads, mine, theirs, merged):
    rank = mine.shape[1] // 2
    half = rank // 2

    @pl.when(leads())
    def _():
        top, other = mine[:rank], theirs[:rank]
        lane = lax.broadcasted_iota(jnp.int32, top.shape, 1)
        merged[:rank] = jnp.where(lane < rank, top + other, top)
        merged[rank : rank + half] = mine[rank : rank + half]
        merged[rank + half : rank + half + 8] = mine[rank + half :] + theirs[rank + half :]
        merged[rank + half + 8 :] = unfold(other, theirs[rank : rank + half])


def inverse_steps(rank):
    least = 2.0 * (DAMP / rank) / (1.0 + 2.0 * DAMP / rank)
    scales = []
    while (1.0 - least) ** 2 > 1e-7:
        image = least * (2.0 - least)
        scales.append(2.0 / (1.0 + image))
        least = scales[-1] * image
    return scales + [1.0]


def inverses(rank, total):
    mixed = total[:rank, :rank]
    turned = mixed.T
    tail = rank + rank // 2
    diag = total[tail : tail + 1, :rank]
    count = total[tail : tail + 1, rank : rank + 1]
    row = lax.broadcasted_iota(jnp.int32, (rank, rank), 0)
    lane = lax.broadcasted_iota(jnp.int32, (rank, rank), 1)
    eye = row == lane
    sum_out = jnp.where(lane <= row, mixed, turned)
    sum_in = jnp.where(lane > row, mixed, jnp.where(eye, diag, turned))
    factor = 2.0 / (1.0 + 2.0 * DAMP / rank)

    def start(sums):
        trace = jnp.sum(jnp.sum(jnp.where(eye, sums, 0.0), axis=0, keepdims=True), axis=1, keepdims=True)
        return sums * (factor / trace) + jnp.where(eye, factor * DAMP / rank, 0.0), factor * count / trace

    t_out, c_out = start(sum_out)
    t_in, c_in = start(sum_in)
    steps = inverse_steps(rank)
    two_eye = jnp.where(eye, 2.0, 0.0)
    x_out = steps[0] * (two_eye - t_out)
    x_in = steps[0] * (two_eye - t_in)
    t_out = steps[0] * (2.0 * t_out - dot_hi(t_out, t_out))
    t_in = steps[0] * (2.0 * t_in - dot_hi(t_in, t_in))
    for n, scale in enumerate(steps[1:]):
        x_out, x_in, p_out, p_in = (
            scale * (2.0 * x_out - dot_hi(x_out, t_out)),
            scale * (2.0 * x_in - dot_hi(x_in, t_in)),
            t_out,
            t_in,
        )
        if n < len(steps) - 2:
            t_out = scale * (2.0 * p_out - dot_hi(p_out, p_out))
            t_in = scale * (2.0 * p_in - dot_hi(p_in, p_in))
    return x_out, x_in, c_out, c_in


def finish_kernel(seq_len, leads, masks, queries, *refs):
    packs, scores = refs[:-1], refs[-1]
    rank = packs[0].shape[1] // 2
    fixed = rank + rank // 2 + 8

    @pl.when(leads())
    def _():
        total = [ref[:fixed] for ref in packs]
        while len(total) > 1:
            total = [total[n] + total[n + 1] for n in range(0, len(total), 2)]
        inv_out, inv_in, c_out, c_in = inverses(rank, total[0])
        pairs = []
        for ref in packs:
            pairs.append(unfold(ref[:rank], ref[rank : rank + rank // 2]))
            if ref.shape[0] > fixed:
                pairs.append(ref[fixed:])
        left = dot_hi(inv_out, pairs[0]) * c_out
        zero = jnp.zeros((rank, rank), jnp.float32)
        right = jnp.concatenate(
            [jnp.concatenate([inv_in, zero], axis=1), jnp.concatenate([zero, inv_in], axis=1)], axis=0
        )
        straight = dot_hi(left, right) * c_in
        crossed = pltpu.roll(straight, rank, 1)
        count = len(pairs)
        sums = [jnp.sum(pair * straight, axis=0, keepdims=True) for pair in pairs]
        sums += [jnp.sum(pair * crossed, axis=0, keepdims=True) for pair in pairs]
        sums = jnp.concatenate(sums, axis=0)
        num = queries.shape[1]
        index = lax.broadcasted_iota(jnp.int32, (2 * count, num), 0) % count
        mask = sum(jnp.where(index == n, value, 0) for n, value in enumerate(masks))
        device = lax.axis_index("dp") ^ mask
        chosen = queries[...]
        second = jnp.where(chosen == 2 * device + 1, jnp.sum(sums[:, :rank], axis=1, keepdims=True), 0.0)
        first = jnp.where(chosen == 2 * device, jnp.sum(sums[:, rank:], axis=1, keepdims=True), 0.0)
        scale = 1.0 / (rank * seq_len)
        scores[0:1, :] = scale * jnp.sum(
            jnp.concatenate([first[:count], second[count:]], axis=0), axis=0, keepdims=True
        )
        scores[1:2, :] = scale * jnp.sum(
            jnp.concatenate([second[:count], first[count:]], axis=0), axis=0, keepdims=True
        )


def shape(*dims):
    return pltpu.VMEM(dims, jnp.float32)


def call(kernel, name, out_shape, *operands):
    return pl.pallas_call(
        kernel,
        out_shape=out_shape,
        in_specs=[VMEM] * len(operands),
        out_specs=VMEM,
        compiler_params=pltpu.CompilerParams(vmem_limit_bytes=4 * 2**20),
        name=name,
    )(*[pltpu.with_memory_space_constraint(operand, pltpu.VMEM) for operand in operands])


def project(activations, out_grads, proj_in, proj_out, lengths):
    examples, seq_len, hidden = activations.shape
    chunks = 7 if hidden % (7 * 128) == 0 else 1
    width = 2 * proj_in.shape[0]
    operands = [lengths, activations, out_grads, proj_in, proj_out]
    return pl.pallas_call(
        project_kernel,
        out_shape=[shape(examples * seq_len, width), shape(8, width)],
        in_specs=[HBM] * 5,
        out_specs=[VMEM] * 2,
        scratch_shapes=[pltpu.SMEM(lengths.shape, jnp.int32)]
        + [pltpu.VMEM(operand.shape, jnp.bfloat16) for operand in operands[1:]]
        + [pltpu.SemaphoreType.DMA((chunks + 2, 2))],
        compiler_params=pltpu.CompilerParams(vmem_limit_bytes=24 * 2**20),
        name="project",
    )(*[pltpu.with_memory_space_constraint(operand, pltpu.HBM) for operand in operands])


def swap(x, dp, tensor, far, near):
    pairs = []
    for d in range(dp):
        for t in range(tensor):
            masks = far if t % 2 else near
            pairs.append((d * tensor + t, (d ^ masks[0]) * tensor + (t ^ masks[1])))
    return lax.ppermute(x, ("dp", "tensor"), pairs)


def per_device(dp, tensor, activations, out_grads, proj_in, proj_out, lengths, query_ids):
    examples, seq_len, _ = activations.shape
    rank = proj_in.shape[1]
    num = query_ids.shape[0]
    paired = dp == 4 and tensor == 4
    odd = lambda: lax.rem(lax.axis_index("tensor"), 2) == 1
    leads = odd if paired else lambda: True
    sketch, live = project(activations, out_grads, proj_in.T, proj_out.T, lengths)
    sketch = sketch + lax.ppermute(sketch, "tensor", [(t, t ^ 1) for t in range(tensor)])
    if paired:
        other = swap(sketch, dp, tensor, (0, 2), (1, 0))
    else:
        other = jnp.zeros_like(sketch)
        step = 2
        while step < tensor:
            sketch = sketch + lax.ppermute(sketch, "tensor", [(t, t ^ step) for t in range(tensor)])
            step *= 2
    packed = call(
        functools.partial(gram_kernel, seq_len, leads),
        "gram",
        shape(rank + rank // 2 + 8, 2 * rank),
        live,
        sketch,
        other,
    )
    if paired:
        other = swap(packed, dp, tensor, (2, 0), (0, 2))
        rows = 2 * rank + rank // 2 + 8
        merged = call(functools.partial(merge_kernel, leads), "merge", shape(rows, 2 * rank), packed, other)
        packs = [merged, swap(merged, dp, tensor, (1, 0), (0, 2))]
        masks = [0, 2, 1, 3]
    else:
        masks = list(range(dp))
        order = lax.axis_index("dp") ^ jnp.arange(dp, dtype=jnp.int32)
        gathered = lax.all_gather(packed, "dp", axis=0)[order]
        packs = [gathered[n] for n in range(dp)]
    scores = call(
        functools.partial(finish_kernel, seq_len, leads, masks),
        "finish",
        shape(examples, num),
        query_ids.reshape(1, num),
        *packs,
    )
    if paired:
        other = lax.ppermute(scores, "tensor", [(t, t ^ 1) for t in range(tensor)])
        scores = jnp.where(odd(), scores, other)
    return scores.T


def solution(mesh):
    placed = (
        P(("groups", "dp"), None, "tensor"),
        P(("groups", "dp"), None, "tensor"),
        P("tensor", None),
        P("tensor", None),
        P(("groups", "dp")),
        P("groups"),
    )
    return jax.shard_map(
        functools.partial(per_device, mesh.shape["dp"], mesh.shape["tensor"]),
        mesh=mesh,
        in_specs=placed,
        out_specs=P(None, ("groups", "dp")),
        check_vma=False,
    )
```

```python
import functools

import jax
import jax.numpy as jnp
from jax import lax
from jax.experimental import pallas as pl
from jax.experimental.pallas import tpu as pltpu
from jax.sharding import PartitionSpec as P

HIGH = lax.Precision.HIGHEST
VMEM = pl.BlockSpec(memory_space=pltpu.VMEM)
HBM = pl.BlockSpec(memory_space=pltpu.HBM)
DAMP = 0.1


def dot_nt(a, b):
    return lax.dot_general(a, b, (((1,), (1,)), ((), ())), preferred_element_type=jnp.float32)


def dot_hi(a, b):
    return jnp.dot(a, b, precision=HIGH, preferred_element_type=jnp.float32)


def project_kernel(lengths, act, grad, proj_in, proj_out, sketch, live, len_s, act_v, grad_v, pin_v, pout_v, out_v, in_v, sems):
    examples, seq_len, hidden = act.shape
    rank = proj_in.shape[0]
    tokens = examples * seq_len
    stages = sems.shape[0] // 2 - 1
    width = hidden // (stages - 1)
    copies = []

    def begin(src, dst):
        copy = pltpu.make_async_copy(src, dst, sems.at[len(copies)])
        copy.start()
        copies.append(copy)

    begin(proj_out, pout_v)
    begin(grad, grad_v)
    for n in range(stages - 1):
        span = pl.ds(n * width, width)
        begin(proj_in.at[:, span], pin_v.at[:, span])
        begin(act.at[:, :, span], act_v.at[:, :, span])
    begin(lengths, len_s)

    def stage(n):
        copies[2 * n].wait()
        copies[2 * n + 1].wait()
        if n == 0:
            out_v[...] = dot_nt(grad_v[...].reshape(tokens, -1), pout_v[...])
            return
        span = pl.ds((n - 1) * width, width)
        in_part = dot_nt(act_v[:, :, span].reshape(tokens, width), pin_v[:, span])
        if n > 1:
            in_part += in_v[...]
        if n < stages - 1:
            in_v[...] = in_part
            return
        both = jnp.concatenate([out_v[...], in_part], axis=1)
        token = lax.broadcasted_iota(jnp.int32, (seq_len, 2 * rank), 0)
        copies[-1].wait()
        count = jnp.int32(0)
        for e in range(examples):
            rows = pl.ds(e * seq_len, seq_len)
            sketch[rows] = jnp.where(token < len_s[e], both[e * seq_len : (e + 1) * seq_len], 0.0)
            count += len_s[e]
        live[...] = jnp.full(live.shape, count.astype(jnp.float32))

    @pl.loop(0, stages)
    def _(turn):
        for n in range(stages):
            pl.when(turn == n)(functools.partial(stage, n))


def gram_kernel(seq_len, leads, live, mine, theirs, packed):
    rank = mine.shape[1] // 2

    @pl.when(leads())
    def _():
        tokens = mine[...] + theirs[...]
        grams = []
        for e in range(2):
            block = tokens[e * seq_len : (e + 1) * seq_len]
            grams.append(
                lax.dot_general(
                    block, block, (((0,), (0,)), ((), ())), precision=HIGH, preferred_element_type=jnp.float32
                )
            )
        total = grams[0] + grams[1]
        low = total[rank:]
        row = lax.broadcasted_iota(jnp.int32, (rank, 2 * rank), 0)
        lane = lax.broadcasted_iota(jnp.int32, (rank, 2 * rank), 1)
        mixed = jnp.where(lane <= row, total[:rank], pltpu.roll(low, rank, 1))
        packed[:rank] = jnp.where(lane < rank, mixed, grams[0][:rank])
        half = rank // 2
        folded = pltpu.roll(grams[1][half:rank], rank, 1)
        packed[rank : rank + half] = jnp.where(lane[:half] < rank, folded, grams[1][:half])
        diag = jnp.sum(jnp.where(lane == rank + row, low, 0.0), axis=0, keepdims=True)
        diag = pltpu.roll(jnp.broadcast_to(diag, (8, 2 * rank)), rank, 1)
        packed[rank + half :] = jnp.where(lane[:8] < rank, diag, live[...])


def unfold(top, folded):
    rank = top.shape[0]
    lane = lax.broadcasted_iota(jnp.int32, top.shape, 1)
    return jnp.where(lane < rank, jnp.concatenate([pltpu.roll(folded, rank, 1), folded], axis=0), top)


def merge_kernel(leads, mine, theirs, merged):
    rank = mine.shape[1] // 2
    half = rank // 2

    @pl.when(leads())
    def _():
        top, other = mine[:rank], theirs[:rank]
        lane = lax.broadcasted_iota(jnp.int32, top.shape, 1)
        merged[:rank] = jnp.where(lane < rank, top + other, top)
        merged[rank : rank + half] = mine[rank : rank + half]
        merged[rank + half : rank + half + 8] = mine[rank + half :] + theirs[rank + half :]
        merged[rank + half + 8 :] = unfold(other, theirs[rank : rank + half])


def inverse_steps(rank):
    least = 2.0 * (DAMP / rank) / (1.0 + 2.0 * DAMP / rank)
    scales = []
    while (1.0 - least) ** 2 > 1e-7:
        image = least * (2.0 - least)
        scales.append(2.0 / (1.0 + image))
        least = scales[-1] * image
    return scales + [1.0]


def inverses(rank, total):
    mixed = total[:rank, :rank]
    turned = mixed.T
    tail = rank + rank // 2
    diag = total[tail : tail + 1, :rank]
    count = total[tail : tail + 1, rank : rank + 1]
    row = lax.broadcasted_iota(jnp.int32, (rank, rank), 0)
    lane = lax.broadcasted_iota(jnp.int32, (rank, rank), 1)
    eye = row == lane
    sum_out = jnp.where(lane <= row, mixed, turned)
    sum_in = jnp.where(lane > row, mixed, jnp.where(eye, diag, turned))
    factor = 2.0 / (1.0 + 2.0 * DAMP / rank)

    def start(sums):
        trace = jnp.sum(jnp.sum(jnp.where(eye, sums, 0.0), axis=0, keepdims=True), axis=1, keepdims=True)
        return sums * (factor / trace) + jnp.where(eye, factor * DAMP / rank, 0.0), factor * count / trace

    t_out, c_out = start(sum_out)
    t_in, c_in = start(sum_in)
    steps = inverse_steps(rank)
    two_eye = jnp.where(eye, 2.0, 0.0)
    x_out = steps[0] * (two_eye - t_out)
    x_in = steps[0] * (two_eye - t_in)
    t_out = steps[0] * (2.0 * t_out - dot_hi(t_out, t_out))
    t_in = steps[0] * (2.0 * t_in - dot_hi(t_in, t_in))
    for n, scale in enumerate(steps[1:]):
        x_out, x_in, p_out, p_in = (
            scale * (2.0 * x_out - dot_hi(x_out, t_out)),
            scale * (2.0 * x_in - dot_hi(x_in, t_in)),
            t_out,
            t_in,
        )
        if n < len(steps) - 2:
            t_out = scale * (2.0 * p_out - dot_hi(p_out, p_out))
            t_in = scale * (2.0 * p_in - dot_hi(p_in, p_in))
    return x_out, x_in, c_out, c_in


def finish_kernel(seq_len, leads, masks, queries, *refs):
    packs, scores = refs[:-1], refs[-1]
    rank = packs[0].shape[1] // 2
    fixed = rank + rank // 2 + 8

    @pl.when(leads())
    def _():
        total = [ref[:fixed] for ref in packs]
        while len(total) > 1:
            total = [total[n] + total[n + 1] for n in range(0, len(total), 2)]
        inv_out, inv_in, c_out, c_in = inverses(rank, total[0])
        pairs = []
        for ref in packs:
            pairs.append(unfold(ref[:rank], ref[rank : rank + rank // 2]))
            if ref.shape[0] > fixed:
                pairs.append(ref[fixed:])
        left = dot_hi(inv_out, pairs[0]) * c_out
        zero = jnp.zeros((rank, rank), jnp.float32)
        right = jnp.concatenate(
            [jnp.concatenate([inv_in, zero], axis=1), jnp.concatenate([zero, inv_in], axis=1)], axis=0
        )
        straight = dot_hi(left, right) * c_in
        crossed = pltpu.roll(straight, rank, 1)
        count = len(pairs)
        sums = [jnp.sum(pair * straight, axis=0, keepdims=True) for pair in pairs]
        sums += [jnp.sum(pair * crossed, axis=0, keepdims=True) for pair in pairs]
        sums = jnp.concatenate(sums, axis=0)
        num = queries.shape[1]
        index = lax.broadcasted_iota(jnp.int32, (2 * count, num), 0) % count
        mask = sum(jnp.where(index == n, value, 0) for n, value in enumerate(masks))
        device = lax.axis_index("dp") ^ mask
        chosen = queries[...]
        second = jnp.where(chosen == 2 * device + 1, jnp.sum(sums[:, :rank], axis=1, keepdims=True), 0.0)
        first = jnp.where(chosen == 2 * device, jnp.sum(sums[:, rank:], axis=1, keepdims=True), 0.0)
        scale = 1.0 / (rank * seq_len)
        scores[0:1, :] = scale * jnp.sum(
            jnp.concatenate([first[:count], second[count:]], axis=0), axis=0, keepdims=True
        )
        scores[1:2, :] = scale * jnp.sum(
            jnp.concatenate([second[:count], first[count:]], axis=0), axis=0, keepdims=True
        )


def shape(*dims):
    return pltpu.VMEM(dims, jnp.float32)


def call(kernel, name, out_shape, *operands):
    return pl.pallas_call(
        kernel,
        out_shape=out_shape,
        in_specs=[VMEM] * len(operands),
        out_specs=VMEM,
        compiler_params=pltpu.CompilerParams(vmem_limit_bytes=4 * 2**20),
        name=name,
    )(*[pltpu.with_memory_space_constraint(operand, pltpu.VMEM) for operand in operands])


def project(activations, out_grads, proj_in, proj_out, lengths):
    examples, seq_len, hidden = activations.shape
    rank = proj_in.shape[0]
    stages = 3 if hidden % 256 == 0 else 2
    operands = [lengths, activations, out_grads, proj_in, proj_out]
    return pl.pallas_call(
        project_kernel,
        out_shape=[shape(examples * seq_len, 2 * rank), shape(8, 2 * rank)],
        in_specs=[HBM] * 5,
        out_specs=[VMEM] * 2,
        scratch_shapes=[pltpu.SMEM(lengths.shape, jnp.int32)]
        + [pltpu.VMEM(operand.shape, jnp.bfloat16) for operand in operands[1:]]
        + [pltpu.VMEM((examples * seq_len, rank), jnp.float32)] * 2
        + [pltpu.SemaphoreType.DMA((2 * stages + 2,))],
        compiler_params=pltpu.CompilerParams(vmem_limit_bytes=24 * 2**20),
        name="project",
    )(*[pltpu.with_memory_space_constraint(operand, pltpu.HBM) for operand in operands])


def swap(x, dp, tensor, far, near):
    pairs = []
    for d in range(dp):
        for t in range(tensor):
            masks = far if t % 2 else near
            pairs.append((d * tensor + t, (d ^ masks[0]) * tensor + (t ^ masks[1])))
    return lax.ppermute(x, ("dp", "tensor"), pairs)


def per_device(dp, tensor, activations, out_grads, proj_in, proj_out, lengths, query_ids):
    examples, seq_len, _ = activations.shape
    rank = proj_in.shape[1]
    num = query_ids.shape[0]
    paired = dp == 4 and tensor == 4
    odd = lambda: lax.rem(lax.axis_index("tensor"), 2) == 1
    leads = odd if paired else lambda: True
    sketch, live = project(activations, out_grads, proj_in.T, proj_out.T, lengths)
    sketch = sketch + lax.ppermute(sketch, "tensor", [(t, t ^ 1) for t in range(tensor)])
    if paired:
        other = swap(sketch, dp, tensor, (0, 2), (1, 0))
    else:
        other = jnp.zeros_like(sketch)
        step = 2
        while step < tensor:
            sketch = sketch + lax.ppermute(sketch, "tensor", [(t, t ^ step) for t in range(tensor)])
            step *= 2
    packed = call(
        functools.partial(gram_kernel, seq_len, leads),
        "gram",
        shape(rank + rank // 2 + 8, 2 * rank),
        live,
        sketch,
        other,
    )
    if paired:
        other = swap(packed, dp, tensor, (2, 0), (0, 2))
        rows = 2 * rank + rank // 2 + 8
        merged = call(functools.partial(merge_kernel, leads), "merge", shape(rows, 2 * rank), packed, other)
        packs = [merged, swap(merged, dp, tensor, (1, 0), (0, 2))]
        masks = [0, 2, 1, 3]
    else:
        masks = list(range(dp))
        order = lax.axis_index("dp") ^ jnp.arange(dp, dtype=jnp.int32)
        gathered = lax.all_gather(packed, "dp", axis=0)[order]
        packs = [gathered[n] for n in range(dp)]
    scores = call(
        functools.partial(finish_kernel, seq_len, leads, masks),
        "finish",
        shape(examples, num),
        query_ids.reshape(1, num),
        *packs,
    )
    if paired:
        other = lax.ppermute(scores, "tensor", [(t, t ^ 1) for t in range(tensor)])
        scores = jnp.where(odd(), scores, other)
    return scores.T


def solution(mesh):
    placed = (
        P(("groups", "dp"), None, "tensor"),
        P(("groups", "dp"), None, "tensor"),
        P("tensor", None),
        P("tensor", None),
        P(("groups", "dp")),
        P("groups"),
    )
    return jax.shard_map(
        functools.partial(per_device, mesh.shape["dp"], mesh.shape["tensor"]),
        mesh=mesh,
        in_specs=placed,
        out_specs=P(None, ("groups", "dp")),
        check_vma=False,
    )
```

```python
import functools

import jax
import jax.numpy as jnp
from jax import lax
from jax.experimental import pallas as pl
from jax.experimental.pallas import tpu as pltpu
from jax.sharding import PartitionSpec as P

HIGH = lax.Precision.HIGHEST
VMEM = pl.BlockSpec(memory_space=pltpu.VMEM)
HBM = pl.BlockSpec(memory_space=pltpu.HBM)
DAMP = 0.1


def dot_nt(a, b):
    return lax.dot_general(a, b, (((1,), (1,)), ((), ())), preferred_element_type=jnp.float32)


def dot_hi(a, b):
    return jnp.dot(a, b, precision=HIGH, preferred_element_type=jnp.float32)


def project_kernel(lengths, act, grad, proj_in, proj_out, sketch, live, len_s, act_v, grad_v, pin_v, pout_v, out_v, in_v, sems):
    examples, seq_len, hidden = act.shape
    rank = proj_in.shape[0]
    tokens = examples * seq_len
    stages = sems.shape[0] // 2 - 1
    width = hidden // (stages - 1)
    copies = []

    def begin(src, dst):
        copy = pltpu.make_async_copy(src, dst, sems.at[len(copies)])
        copy.start()
        copies.append(copy)

    begin(proj_out, pout_v)
    begin(grad, grad_v)
    for n in range(stages - 1):
        span = pl.ds(n * width, width)
        begin(proj_in.at[:, span], pin_v.at[:, span])
        begin(act.at[:, :, span], act_v.at[:, :, span])
    begin(lengths, len_s)

    def stage(n):
        copies[2 * n].wait()
        copies[2 * n + 1].wait()
        if n == 0:
            out_v[...] = dot_nt(grad_v[...].reshape(tokens, -1), pout_v[...])
            return
        span = pl.ds((n - 1) * width, width)
        in_part = dot_nt(act_v[:, :, span].reshape(tokens, width), pin_v[:, span])
        if n > 1:
            in_part += in_v[...]
        if n < stages - 1:
            in_v[...] = in_part
            return
        both = jnp.concatenate([out_v[...], in_part], axis=1)
        token = lax.broadcasted_iota(jnp.int32, (seq_len, 2 * rank), 0)
        copies[-1].wait()
        count = jnp.int32(0)
        for e in range(examples):
            rows = pl.ds(e * seq_len, seq_len)
            sketch[rows] = jnp.where(token < len_s[e], both[e * seq_len : (e + 1) * seq_len], 0.0)
            count += len_s[e]
        live[...] = jnp.full(live.shape, count.astype(jnp.float32))

    @pl.loop(0, stages)
    def _(turn):
        for n in range(stages):
            pl.when(turn == n)(functools.partial(stage, n))


def gram_kernel(seq_len, leads, live, mine, theirs, packed):
    rank = mine.shape[1] // 2

    @pl.when(leads())
    def _():
        tokens = mine[...] + theirs[...]
        grams = []
        for e in range(2):
            block = tokens[e * seq_len : (e + 1) * seq_len]
            grams.append(
                lax.dot_general(
                    block, block, (((0,), (0,)), ((), ())), precision=HIGH, preferred_element_type=jnp.float32
                )
            )
        total = grams[0] + grams[1]
        low = total[rank:]
        row = lax.broadcasted_iota(jnp.int32, (rank, 2 * rank), 0)
        lane = lax.broadcasted_iota(jnp.int32, (rank, 2 * rank), 1)
        mixed = jnp.where(lane <= row, total[:rank], pltpu.roll(low, rank, 1))
        packed[:rank] = jnp.where(lane < rank, mixed, grams[0][:rank])
        half = rank // 2
        folded = pltpu.roll(grams[1][half:rank], rank, 1)
        packed[rank : rank + half] = jnp.where(lane[:half] < rank, folded, grams[1][:half])
        diag = jnp.sum(jnp.where(lane == rank + row, low, 0.0), axis=0, keepdims=True)
        diag = pltpu.roll(jnp.broadcast_to(diag, (8, 2 * rank)), rank, 1)
        packed[rank + half :] = jnp.where(lane[:8] < rank, diag, live[...])


def unfold(top, folded):
    rank = top.shape[0]
    lane = lax.broadcasted_iota(jnp.int32, top.shape, 1)
    return jnp.where(lane < rank, jnp.concatenate([pltpu.roll(folded, rank, 1), folded], axis=0), top)


def merge_kernel(leads, mine, theirs, merged):
    rank = mine.shape[1] // 2
    half = rank // 2

    @pl.when(leads())
    def _():
        top, other = mine[:rank], theirs[:rank]
        lane = lax.broadcasted_iota(jnp.int32, top.shape, 1)
        merged[:rank] = jnp.where(lane < rank, top + other, top)
        merged[rank : rank + half] = mine[rank : rank + half]
        merged[rank + half : rank + half + 8] = mine[rank + half :] + theirs[rank + half :]
        merged[rank + half + 8 :] = unfold(other, theirs[rank : rank + half])


def inverse_steps(rank):
    least = 2.0 * (DAMP / rank) / (1.0 + 2.0 * DAMP / rank)
    scales = []
    while (1.0 - least) ** 2 > 1e-7:
        image = least * (2.0 - least)
        scales.append(2.0 / (1.0 + image))
        least = scales[-1] * image
    return scales + [1.0]


def scaled(rank, total):
    mixed = total[:rank, :rank]
    turned = mixed.T
    tail = rank + rank // 2
    diag = total[tail : tail + 1, :rank]
    count = total[tail : tail + 1, rank : rank + 1]
    row = lax.broadcasted_iota(jnp.int32, (rank, rank), 0)
    lane = lax.broadcasted_iota(jnp.int32, (rank, rank), 1)
    eye = row == lane
    sum_out = jnp.where(lane <= row, mixed, turned)
    sum_in = jnp.where(lane > row, mixed, jnp.where(eye, diag, turned))
    factor = 2.0 / (1.0 + 2.0 * DAMP / rank)

    def scale(sums):
        trace = jnp.sum(jnp.sum(jnp.where(eye, sums, 0.0), axis=0, keepdims=True), axis=1, keepdims=True)
        return sums * (factor / trace) + jnp.where(eye, factor * DAMP / rank, 0.0), factor * count / trace

    return *scale(sum_out), *scale(sum_in), jnp.where(eye, 2.0, 0.0)


def solve(rank, total, right):
    t_out, c_out, t_in, c_in, two_eye = scaled(rank, total)
    steps = inverse_steps(rank)
    x_in = steps[0] * (two_eye - t_in)
    for n, scale in enumerate(steps):
        last = n == len(steps) - 1
        p_out, p_in = t_out, t_in
        right = scale * (2.0 * right - dot_hi(p_out, right))
        if not last:
            t_out = scale * (2.0 * p_out - dot_hi(p_out, p_out))
        if n > 0:
            x_in = scale * (2.0 * x_in - dot_hi(x_in, p_in))
        if not last:
            t_in = scale * (2.0 * p_in - dot_hi(p_in, p_in))
    return right, x_in, c_out, c_in


def finish_kernel(seq_len, leads, masks, queries, *refs):
    packs, scores = refs[:-1], refs[-1]
    rank = packs[0].shape[1] // 2
    fixed = rank + rank // 2 + 8

    @pl.when(leads())
    def _():
        total = [ref[:fixed] for ref in packs]
        while len(total) > 1:
            total = [total[n] + total[n + 1] for n in range(0, len(total), 2)]
        pairs = []
        for ref in packs:
            pairs.append(unfold(ref[:rank], ref[rank : rank + rank // 2]))
            if ref.shape[0] > fixed:
                pairs.append(ref[fixed:])
        left, inv_in, c_out, c_in = solve(rank, total[0], pairs[0])
        left = left * c_out
        zero = jnp.zeros((rank, rank), jnp.float32)
        right = jnp.concatenate(
            [jnp.concatenate([inv_in, zero], axis=1), jnp.concatenate([zero, inv_in], axis=1)], axis=0
        )
        straight = dot_hi(left, right) * c_in
        crossed = pltpu.roll(straight, rank, 1)
        count = len(pairs)
        sums = [jnp.sum(pair * straight, axis=0, keepdims=True) for pair in pairs]
        sums += [jnp.sum(pair * crossed, axis=0, keepdims=True) for pair in pairs]
        sums = jnp.concatenate(sums, axis=0)
        num = queries.shape[1]
        index = lax.broadcasted_iota(jnp.int32, (2 * count, num), 0) % count
        mask = sum(jnp.where(index == n, value, 0) for n, value in enumerate(masks))
        device = lax.axis_index("dp") ^ mask
        chosen = queries[...]
        second = jnp.where(chosen == 2 * device + 1, jnp.sum(sums[:, :rank], axis=1, keepdims=True), 0.0)
        first = jnp.where(chosen == 2 * device, jnp.sum(sums[:, rank:], axis=1, keepdims=True), 0.0)
        scale = 1.0 / (rank * seq_len)
        scores[0:1, :] = scale * jnp.sum(
            jnp.concatenate([first[:count], second[count:]], axis=0), axis=0, keepdims=True
        )
        scores[1:2, :] = scale * jnp.sum(
            jnp.concatenate([second[:count], first[count:]], axis=0), axis=0, keepdims=True
        )


def publish_kernel(scores, out, sem):
    copy = pltpu.make_async_copy(scores, out, sem)
    copy.start()
    copy.wait()


def replace_kernel(leads, theirs, mine, out, sem):
    @pl.when(jnp.logical_not(leads()))
    def _():
        copy = pltpu.make_async_copy(theirs, out, sem)
        copy.start()
        copy.wait()


def shape(*dims):
    return pltpu.VMEM(dims, jnp.float32)


def call(kernel, name, out_shape, *operands):
    return pl.pallas_call(
        kernel,
        out_shape=out_shape,
        in_specs=[VMEM] * len(operands),
        out_specs=VMEM,
        compiler_params=pltpu.CompilerParams(vmem_limit_bytes=4 * 2**20),
        name=name,
    )(*[pltpu.with_memory_space_constraint(operand, pltpu.VMEM) for operand in operands])


def project(activations, out_grads, proj_in, proj_out, lengths):
    examples, seq_len, hidden = activations.shape
    rank = proj_in.shape[0]
    stages = 3 if hidden % 256 == 0 else 2
    operands = [lengths, activations, out_grads, proj_in, proj_out]
    return pl.pallas_call(
        project_kernel,
        out_shape=[shape(examples * seq_len, 2 * rank), shape(8, 2 * rank)],
        in_specs=[HBM] * 5,
        out_specs=[VMEM] * 2,
        scratch_shapes=[pltpu.SMEM(lengths.shape, jnp.int32)]
        + [pltpu.VMEM(operand.shape, jnp.bfloat16) for operand in operands[1:]]
        + [pltpu.VMEM((examples * seq_len, rank), jnp.float32)] * 2
        + [pltpu.SemaphoreType.DMA((2 * stages + 2,))],
        compiler_params=pltpu.CompilerParams(vmem_limit_bytes=24 * 2**20),
        name="project",
    )(*[pltpu.with_memory_space_constraint(operand, pltpu.HBM) for operand in operands])


def swap(x, dp, tensor, far, near):
    pairs = []
    for d in range(dp):
        for t in range(tensor):
            masks = far if t % 2 else near
            pairs.append((d * tensor + t, (d ^ masks[0]) * tensor + (t ^ masks[1])))
    return lax.ppermute(x, ("dp", "tensor"), pairs)


def across(x, tensor):
    return lax.ppermute(x, "tensor", [(t, t ^ 1) for t in range(tensor)])


def publish(scores):
    return pl.pallas_call(
        publish_kernel,
        out_shape=jax.ShapeDtypeStruct(scores.shape, scores.dtype),
        in_specs=[VMEM],
        out_specs=HBM,
        scratch_shapes=[pltpu.SemaphoreType.DMA],
        compiler_params=pltpu.CompilerParams(vmem_limit_bytes=2**20),
        cost_estimate=pl.CostEstimate(flops=10**9, bytes_accessed=0, transcendentals=0),
        name="publish",
    )(pltpu.with_memory_space_constraint(scores, pltpu.VMEM))


def replace(theirs, mine, leads):
    return pl.pallas_call(
        functools.partial(replace_kernel, leads),
        out_shape=jax.ShapeDtypeStruct(mine.shape, mine.dtype),
        in_specs=[VMEM, HBM],
        out_specs=HBM,
        scratch_shapes=[pltpu.SemaphoreType.DMA],
        input_output_aliases={1: 0},
        compiler_params=pltpu.CompilerParams(vmem_limit_bytes=2**20),
        name="replace",
    )(pltpu.with_memory_space_constraint(theirs, pltpu.VMEM), mine)


def per_device(dp, tensor, activations, out_grads, proj_in, proj_out, lengths, query_ids):
    examples, seq_len, _ = activations.shape
    rank = proj_in.shape[1]
    num = query_ids.shape[0]
    paired = dp == 4 and tensor == 4
    odd = lambda: lax.rem(lax.axis_index("tensor"), 2) == 1
    leads = odd if paired else lambda: True
    sketch, live = project(activations, out_grads, proj_in.T, proj_out.T, lengths)
    sketch = sketch + across(sketch, tensor)
    if paired:
        other = swap(sketch, dp, tensor, (0, 2), (1, 0))
    else:
        other = jnp.zeros_like(sketch)
        step = 2
        while step < tensor:
            sketch = sketch + lax.ppermute(sketch, "tensor", [(t, t ^ step) for t in range(tensor)])
            step *= 2
    packed = call(
        functools.partial(gram_kernel, seq_len, leads),
        "gram",
        shape(rank + rank // 2 + 8, 2 * rank),
        live,
        sketch,
        other,
    )
    if paired:
        other = swap(packed, dp, tensor, (2, 0), (0, 2))
        rows = 2 * rank + rank // 2 + 8
        merged = call(functools.partial(merge_kernel, leads), "merge", shape(rows, 2 * rank), packed, other)
        packs = [merged, swap(merged, dp, tensor, (1, 0), (0, 2))]
        masks = [0, 2, 1, 3]
    else:
        masks = list(range(dp))
        order = lax.axis_index("dp") ^ jnp.arange(dp, dtype=jnp.int32)
        gathered = lax.all_gather(packed, "dp", axis=0)[order]
        packs = [gathered[n] for n in range(dp)]
    scores = call(
        functools.partial(finish_kernel, seq_len, leads, masks),
        "finish",
        shape(examples, num),
        query_ids.reshape(1, num),
        *packs,
    )
    if paired:
        other = across(scores, tensor)
        scores = replace(other, publish(scores), leads)
    return scores.T


def solution(mesh):
    placed = (
        P(("groups", "dp"), None, "tensor"),
        P(("groups", "dp"), None, "tensor"),
        P("tensor", None),
        P("tensor", None),
        P(("groups", "dp")),
        P("groups"),
    )
    return jax.shard_map(
        functools.partial(per_device, mesh.shape["dp"], mesh.shape["tensor"]),
        mesh=mesh,
        in_specs=placed,
        out_specs=P(None, ("groups", "dp")),
        check_vma=False,
    )
```

```python
import functools

import jax
import jax.numpy as jnp
from jax import lax
from jax.experimental import pallas as pl
from jax.experimental.pallas import tpu as pltpu
from jax.sharding import PartitionSpec as P

HIGH = lax.Precision.HIGHEST
VMEM = pl.BlockSpec(memory_space=pltpu.VMEM)
HBM = pl.BlockSpec(memory_space=pltpu.HBM)
DAMP = 0.1


def dot_nt(a, b):
    return lax.dot_general(a, b, (((1,), (1,)), ((), ())), preferred_element_type=jnp.float32)


def dot_hi(a, b):
    return jnp.dot(a, b, precision=HIGH, preferred_element_type=jnp.float32)


def project_kernel(lengths, act, grad, proj_in, proj_out, sketch, live, len_s, act_v, grad_v, pin_v, pout_v, out_v, in_v, sems):
    examples, seq_len, hidden = act.shape
    rank = proj_in.shape[0]
    tokens = examples * seq_len
    stages = sems.shape[0] // 2 - 1
    width = hidden // (stages - 1)
    copies = []

    def begin(src, dst):
        copy = pltpu.make_async_copy(src, dst, sems.at[len(copies)])
        copy.start()
        copies.append(copy)

    begin(proj_out, pout_v)
    begin(grad, grad_v)
    for n in range(stages - 1):
        span = pl.ds(n * width, width)
        begin(proj_in.at[:, span], pin_v.at[:, span])
        begin(act.at[:, :, span], act_v.at[:, :, span])
    begin(lengths, len_s)

    def stage(n):
        copies[2 * n].wait()
        copies[2 * n + 1].wait()
        if n == 0:
            out_v[...] = dot_nt(grad_v[...].reshape(tokens, -1), pout_v[...])
            return
        span = pl.ds((n - 1) * width, width)
        in_part = dot_nt(act_v[:, :, span].reshape(tokens, width), pin_v[:, span])
        if n > 1:
            in_part += in_v[...]
        if n < stages - 1:
            in_v[...] = in_part
            return
        both = jnp.concatenate([out_v[...], in_part], axis=1)
        token = lax.broadcasted_iota(jnp.int32, (seq_len, 2 * rank), 0)
        copies[-1].wait()
        count = jnp.int32(0)
        for e in range(examples):
            rows = pl.ds(e * seq_len, seq_len)
            sketch[rows] = jnp.where(token < len_s[e], both[e * seq_len : (e + 1) * seq_len], 0.0)
            count += len_s[e]
        live[...] = jnp.full(live.shape, count.astype(jnp.float32))

    @pl.loop(0, stages)
    def _(turn):
        for n in range(stages):
            pl.when(turn == n)(functools.partial(stage, n))


def gram_kernel(seq_len, leads, live, mine, theirs, packed):
    rank = mine.shape[1] // 2
    half = rank // 2

    @pl.when(leads())
    def _():
        tokens = mine[...] + theirs[...]
        grams = []
        for e in range(2):
            block = tokens[e * seq_len : (e + 1) * seq_len]
            grams.append(
                lax.dot_general(
                    block, block, (((0,), (0,)), ((), ())), precision=HIGH, preferred_element_type=jnp.float32
                )
            )
        total = grams[0] + grams[1]
        high, low = total[:rank], total[rank:]
        row = lax.broadcasted_iota(jnp.int32, (half, 2 * rank), 0)
        lane = lax.broadcasted_iota(jnp.int32, (half, 2 * rank), 1)
        packed[rank : rank + half] = jnp.where(
            lane < rank,
            jnp.where(lane <= row, high[:half], pltpu.roll(low[:half], rank, 1)),
            jnp.where(lane - rank <= row + half, pltpu.roll(high[half:], rank, 1), low[half:]),
        )
        row = lax.broadcasted_iota(jnp.int32, (rank, 2 * rank), 0)
        lane = lax.broadcasted_iota(jnp.int32, (rank, 2 * rank), 1)
        diag = jnp.sum(jnp.where(lane == rank + row, low, 0.0), axis=0, keepdims=True)
        packed[rank + half :] = jnp.where(lane[:8] < rank, live[...], diag)
        packed[:rank] = jnp.where(lane < rank, pltpu.roll(grams[1][:rank], rank, 1), grams[0][:rank])


def merge_kernel(leads, mine, theirs, merged):
    rank = mine.shape[1] // 2

    @pl.when(leads())
    def _():
        merged[:rank] = theirs[:rank]
        merged[rank:] = mine[rank:] + theirs[rank:]


def inverse_steps(rank):
    least = 2.0 * (DAMP / rank) / (1.0 + 2.0 * DAMP / rank)
    scales = []
    while (1.0 - least) ** 2 > 1e-7:
        image = least * (2.0 - least)
        scales.append(2.0 / (1.0 + image))
        least = scales[-1] * image
    return scales + [1.0]


def scaled(rank, total):
    half = rank // 2
    mixed = jnp.concatenate([total[:half, :rank], total[:half, rank:]], axis=0)
    turned = mixed.T
    diag = total[half : half + 1, rank:]
    count = total[half : half + 1, :1]
    row = lax.broadcasted_iota(jnp.int32, (rank, rank), 0)
    lane = lax.broadcasted_iota(jnp.int32, (rank, rank), 1)
    eye = row == lane
    sum_out = jnp.where(lane <= row, mixed, turned)
    sum_in = jnp.where(lane > row, mixed, jnp.where(eye, diag, turned))
    factor = 2.0 / (1.0 + 2.0 * DAMP / rank)

    def scale(sums):
        trace = jnp.sum(jnp.sum(jnp.where(eye, sums, 0.0), axis=0, keepdims=True), axis=1, keepdims=True)
        return sums * (factor / trace) + jnp.where(eye, factor * DAMP / rank, 0.0), factor * count / trace

    return *scale(sum_out), *scale(sum_in), jnp.where(eye, 2.0, 0.0)


def solve(rank, total, right):
    t_out, c_out, t_in, c_in, two_eye = scaled(rank, total)
    steps = inverse_steps(rank)
    x_in = steps[0] * (two_eye - t_in)
    for n, scale in enumerate(steps):
        last = n == len(steps) - 1
        p_out, p_in = t_out, t_in
        right = scale * (2.0 * right - dot_hi(p_out, right))
        if not last:
            t_out = scale * (2.0 * p_out - dot_hi(p_out, p_out))
        if n > 0:
            x_in = scale * (2.0 * x_in - dot_hi(x_in, p_in))
        if not last:
            t_in = scale * (2.0 * p_in - dot_hi(p_in, p_in))
    return right, x_in, c_out, c_in


def finish_kernel(seq_len, leads, masks, count, queries, *refs):
    blocks, scores = refs[:-1], refs[-1]
    rank = blocks[0].shape[1] // 2

    @pl.when(leads())
    def _():
        pairs = [ref[:rank] for ref in blocks]
        total = [ref[rank:] for ref in blocks[:count]]
        while len(total) > 1:
            total = [total[n] + total[n + 1] for n in range(0, len(total), 2)]
        left, inv_in, c_out, c_in = solve(rank, total[0], pairs[masks.index(0)])
        left = left * c_out
        zero = jnp.zeros((rank, rank), jnp.float32)
        right = jnp.concatenate(
            [jnp.concatenate([inv_in, zero], axis=1), jnp.concatenate([zero, inv_in], axis=1)], axis=0
        )
        straight = dot_hi(left, right) * c_in
        crossed = pltpu.roll(straight, rank, 1)
        size = len(pairs)
        sums = [jnp.sum(pair * straight, axis=0, keepdims=True) for pair in pairs]
        sums += [jnp.sum(pair * crossed, axis=0, keepdims=True) for pair in pairs]
        sums = jnp.concatenate(sums, axis=0)
        num = queries.shape[1]
        index = lax.broadcasted_iota(jnp.int32, (2 * size, num), 0) % size
        mask = sum(jnp.where(index == n, value, 0) for n, value in enumerate(masks))
        device = lax.axis_index("dp") ^ mask
        chosen = queries[...]
        second = jnp.where(chosen == 2 * device + 1, jnp.sum(sums[:, :rank], axis=1, keepdims=True), 0.0)
        first = jnp.where(chosen == 2 * device, jnp.sum(sums[:, rank:], axis=1, keepdims=True), 0.0)
        scale = 1.0 / (rank * seq_len)
        scores[0:1, :] = scale * jnp.sum(
            jnp.concatenate([first[:size], second[size:]], axis=0), axis=0, keepdims=True
        )
        scores[1:2, :] = scale * jnp.sum(
            jnp.concatenate([second[:size], first[size:]], axis=0), axis=0, keepdims=True
        )


def publish_kernel(scores, out, sem):
    copy = pltpu.make_async_copy(scores, out, sem)
    copy.start()
    copy.wait()


def replace_kernel(leads, theirs, mine, out, sem):
    @pl.when(jnp.logical_not(leads()))
    def _():
        copy = pltpu.make_async_copy(theirs, out, sem)
        copy.start()
        copy.wait()


def shape(*dims):
    return pltpu.VMEM(dims, jnp.float32)


def call(kernel, name, out_shape, *operands):
    return pl.pallas_call(
        kernel,
        out_shape=out_shape,
        in_specs=[VMEM] * len(operands),
        out_specs=VMEM,
        compiler_params=pltpu.CompilerParams(vmem_limit_bytes=4 * 2**20),
        name=name,
    )(*[pltpu.with_memory_space_constraint(operand, pltpu.VMEM) for operand in operands])


def project(activations, out_grads, proj_in, proj_out, lengths):
    examples, seq_len, hidden = activations.shape
    rank = proj_in.shape[0]
    stages = 3 if hidden % 256 == 0 else 2
    operands = [lengths, activations, out_grads, proj_in, proj_out]
    return pl.pallas_call(
        project_kernel,
        out_shape=[shape(examples * seq_len, 2 * rank), shape(8, 2 * rank)],
        in_specs=[HBM] * 5,
        out_specs=[VMEM] * 2,
        scratch_shapes=[pltpu.SMEM(lengths.shape, jnp.int32)]
        + [pltpu.VMEM(operand.shape, jnp.bfloat16) for operand in operands[1:]]
        + [pltpu.VMEM((examples * seq_len, rank), jnp.float32)] * 2
        + [pltpu.SemaphoreType.DMA((2 * stages + 2,))],
        compiler_params=pltpu.CompilerParams(vmem_limit_bytes=24 * 2**20),
        name="project",
    )(*[pltpu.with_memory_space_constraint(operand, pltpu.HBM) for operand in operands])


def swap(x, dp, tensor, far, near):
    pairs = []
    for d in range(dp):
        for t in range(tensor):
            masks = far if t % 2 else near
            pairs.append((d * tensor + t, (d ^ masks[0]) * tensor + (t ^ masks[1])))
    return lax.ppermute(x, ("dp", "tensor"), pairs)


def across(x, tensor):
    return lax.ppermute(x, "tensor", [(t, t ^ 1) for t in range(tensor)])


def publish(scores):
    return pl.pallas_call(
        publish_kernel,
        out_shape=jax.ShapeDtypeStruct(scores.shape, scores.dtype),
        in_specs=[VMEM],
        out_specs=HBM,
        scratch_shapes=[pltpu.SemaphoreType.DMA],
        compiler_params=pltpu.CompilerParams(vmem_limit_bytes=2**20),
        cost_estimate=pl.CostEstimate(flops=10**9, bytes_accessed=0, transcendentals=0),
        name="publish",
    )(pltpu.with_memory_space_constraint(scores, pltpu.VMEM))


def replace(theirs, mine, leads):
    return pl.pallas_call(
        functools.partial(replace_kernel, leads),
        out_shape=jax.ShapeDtypeStruct(mine.shape, mine.dtype),
        in_specs=[VMEM, HBM],
        out_specs=HBM,
        scratch_shapes=[pltpu.SemaphoreType.DMA],
        input_output_aliases={1: 0},
        compiler_params=pltpu.CompilerParams(vmem_limit_bytes=2**20),
        name="replace",
    )(pltpu.with_memory_space_constraint(theirs, pltpu.VMEM), mine)


def per_device(dp, tensor, activations, out_grads, proj_in, proj_out, lengths, query_ids):
    examples, seq_len, _ = activations.shape
    rank = proj_in.shape[1]
    num = query_ids.shape[0]
    paired = dp == 4 and tensor == 4
    odd = lambda: lax.rem(lax.axis_index("tensor"), 2) == 1
    leads = odd if paired else lambda: True
    sketch, live = project(activations, out_grads, proj_in.T, proj_out.T, lengths)
    sketch = sketch + across(sketch, tensor)
    if paired:
        other = swap(sketch, dp, tensor, (0, 2), (1, 0))
    else:
        other = jnp.zeros_like(sketch)
        step = 2
        while step < tensor:
            sketch = sketch + lax.ppermute(sketch, "tensor", [(t, t ^ step) for t in range(tensor)])
            step *= 2
    packed = call(
        functools.partial(gram_kernel, seq_len, leads),
        "gram",
        shape(rank + rank // 2 + 8, 2 * rank),
        live,
        sketch,
        other,
    )
    if paired:
        own = packed
        near = swap(packed, dp, tensor, (1, 0), (0, 2))
        other = swap(packed, dp, tensor, (2, 0), (0, 2))
        merged = call(
            functools.partial(merge_kernel, leads), "merge", shape(rank + rank // 2 + 8, 2 * rank), packed, other
        )
        blocks = [merged, swap(merged, dp, tensor, (1, 0), (0, 2)), own, near]
        masks = [2, 3, 0, 1]
        count = 2
    else:
        masks = list(range(dp))
        count = dp
        order = lax.axis_index("dp") ^ jnp.arange(dp, dtype=jnp.int32)
        gathered = lax.all_gather(packed, "dp", axis=0)[order]
        blocks = [gathered[n] for n in range(dp)]
    scores = call(
        functools.partial(finish_kernel, seq_len, leads, masks, count),
        "finish",
        shape(examples, num),
        query_ids.reshape(1, num),
        *blocks,
    )
    if paired:
        other = across(scores, tensor)
        scores = replace(other, publish(scores), leads)
    return scores.T


def solution(mesh):
    placed = (
        P(("groups", "dp"), None, "tensor"),
        P(("groups", "dp"), None, "tensor"),
        P("tensor", None),
        P("tensor", None),
        P(("groups", "dp")),
        P("groups"),
    )
    return jax.shard_map(
        functools.partial(per_device, mesh.shape["dp"], mesh.shape["tensor"]),
        mesh=mesh,
        in_specs=placed,
        out_specs=P(None, ("groups", "dp")),
        check_vma=False,
    )
```

```python
import functools

import jax
import jax.numpy as jnp
from jax import lax
from jax.experimental import pallas as pl
from jax.experimental.pallas import tpu as pltpu
from jax.sharding import PartitionSpec as P

HIGH = lax.Precision.HIGHEST
VMEM = pl.BlockSpec(memory_space=pltpu.VMEM)
HBM = pl.BlockSpec(memory_space=pltpu.HBM)
DAMP = 0.1
STEPS = 5


def dot_nt(a, b):
    return lax.dot_general(a, b, (((1,), (1,)), ((), ())), preferred_element_type=jnp.float32)


def dot_hi(a, b):
    return jnp.dot(a, b, precision=HIGH, preferred_element_type=jnp.float32)


def project_kernel(lengths, act, grad, proj_in, proj_out, sketch, live, len_s, act_v, grad_v, pin_v, pout_v, out_v, in_v, sems):
    examples, seq_len, hidden = act.shape
    rank = proj_in.shape[0]
    tokens = examples * seq_len
    stages = sems.shape[0] // 2 - 1
    width = hidden // (stages - 1)
    copies = []

    def begin(src, dst):
        copy = pltpu.make_async_copy(src, dst, sems.at[len(copies)])
        copy.start()
        copies.append(copy)

    begin(proj_out, pout_v)
    begin(grad, grad_v)
    for n in range(stages - 1):
        span = pl.ds(n * width, width)
        begin(proj_in.at[:, span], pin_v.at[:, span])
        begin(act.at[:, :, span], act_v.at[:, :, span])
    begin(lengths, len_s)

    def stage(n):
        copies[2 * n].wait()
        copies[2 * n + 1].wait()
        if n == 0:
            out_v[...] = dot_nt(grad_v[...].reshape(tokens, -1), pout_v[...])
            return
        span = pl.ds((n - 1) * width, width)
        in_part = dot_nt(act_v[:, :, span].reshape(tokens, width), pin_v[:, span])
        if n > 1:
            in_part += in_v[...]
        if n < stages - 1:
            in_v[...] = in_part
            return
        both = jnp.concatenate([out_v[...], in_part], axis=1)
        token = lax.broadcasted_iota(jnp.int32, (seq_len, 2 * rank), 0)
        copies[-1].wait()
        count = jnp.int32(0)
        for e in range(examples):
            rows = pl.ds(e * seq_len, seq_len)
            sketch[rows] = jnp.where(token < len_s[e], both[e * seq_len : (e + 1) * seq_len], 0.0)
            count += len_s[e]
        live[...] = jnp.full(live.shape, count.astype(jnp.float32))

    @pl.loop(0, stages)
    def _(turn):
        for n in range(stages):
            pl.when(turn == n)(functools.partial(stage, n))


def gram_kernel(seq_len, leads, live, mine, theirs, packed):
    rank = mine.shape[1] // 2
    half = rank // 2

    @pl.when(leads())
    def _():
        tokens = mine[...] + theirs[...]
        grams = []
        for e in range(2):
            block = tokens[e * seq_len : (e + 1) * seq_len]
            grams.append(
                lax.dot_general(
                    block, block, (((0,), (0,)), ((), ())), precision=HIGH, preferred_element_type=jnp.float32
                )
            )
        total = grams[0] + grams[1]
        high, low = total[:rank], total[rank:]
        row = lax.broadcasted_iota(jnp.int32, (half, 2 * rank), 0)
        lane = lax.broadcasted_iota(jnp.int32, (half, 2 * rank), 1)
        packed[rank : rank + half] = jnp.where(
            lane < rank,
            jnp.where(lane <= row, high[:half], pltpu.roll(low[:half], rank, 1)),
            jnp.where(lane - rank <= row + half, pltpu.roll(high[half:], rank, 1), low[half:]),
        )
        row = lax.broadcasted_iota(jnp.int32, (rank, 2 * rank), 0)
        lane = lax.broadcasted_iota(jnp.int32, (rank, 2 * rank), 1)
        diag = jnp.sum(jnp.where(lane == rank + row, low, 0.0), axis=0, keepdims=True)
        packed[rank + half :] = jnp.where(lane[:8] < rank, live[...], diag)
        packed[:rank] = jnp.where(lane < rank, pltpu.roll(grams[1][:rank], rank, 1), grams[0][:rank])


def merge_kernel(leads, mine, theirs, merged):
    rank = mine.shape[1] // 2

    @pl.when(leads())
    def _():
        merged[:rank] = theirs[:rank]
        merged[rank:] = mine[rank:] + theirs[rank:]


def normalised(rank, total):
    half = rank // 2
    mixed = jnp.concatenate([total[:half, :rank], total[:half, rank:]], axis=0)
    turned = mixed.T
    diag = total[half : half + 1, rank:]
    count = total[half : half + 1, :1]
    row = lax.broadcasted_iota(jnp.int32, (rank, rank), 0)
    lane = lax.broadcasted_iota(jnp.int32, (rank, rank), 1)
    eye = row == lane
    sum_out = jnp.where(lane <= row, mixed, turned)
    sum_in = jnp.where(lane > row, mixed, jnp.where(eye, diag, turned))

    def divide(sums):
        trace = jnp.sum(jnp.sum(jnp.where(eye, sums, 0.0), axis=0, keepdims=True), axis=1, keepdims=True)
        return sums / trace + jnp.where(eye, DAMP / rank, 0.0), count / trace

    return *divide(sum_out), *divide(sum_in), jnp.where(eye, 1.0, 0.0)


def total_square(matrix):
    return jnp.sum(jnp.sum(matrix * matrix, axis=0, keepdims=True), axis=1, keepdims=True)


def solve(rank, total, right):
    d_out, c_out, d_in, c_in, eye = normalised(rank, total)

    def scale(matrix):
        mean = (1.0 + DAMP) / rank
        spread = jnp.sqrt(jnp.maximum(total_square(matrix) / rank - mean * mean, 0.0))
        return 2.0 / (mean + spread * (rank - 1) ** 0.5 + DAMP / rank)

    s_out, s_in = scale(d_out), scale(d_in)
    t_out = s_out * (2.0 * d_out - s_out * dot_hi(d_out, d_out))
    t_in = s_in * (2.0 * d_in - s_in * dot_hi(d_in, d_in))
    right = 2.0 * right - s_out * dot_hi(d_out, right)
    x_in = 2.0 * eye - s_in * d_in

    def square(t_out, t_in):
        return 2.0 * t_out - dot_hi(t_out, t_out), 2.0 * t_in - dot_hi(t_in, t_in)

    def update(t_out, t_in, right, x_in):
        return 2.0 * right - dot_hi(t_out, right), 2.0 * x_in - dot_hi(x_in, t_in)

    def residual(t_out, t_in):
        return jnp.sum(total_square(eye - t_out) + total_square(eye - t_in))

    for n in range(STEPS - 1):
        right, x_in = update(t_out, t_in, right, x_in)
        if n < STEPS - 2:
            t_out, t_in = square(t_out, t_in)

    def unfinished(state):
        return jnp.logical_and(state[0] > 1e-5, state[1] < 40)

    def more(state):
        _, n, t_out, t_in, right, x_in = state
        t_out, t_in = square(t_out, t_in)
        right, x_in = update(t_out, t_in, right, x_in)
        return residual(t_out, t_in), n + 1, t_out, t_in, right, x_in

    state = (residual(t_out, t_in), jnp.int32(0), t_out, t_in, right, x_in)
    _, _, _, _, right, x_in = lax.while_loop(unfinished, more, state)
    return right, x_in, c_out * s_out, c_in * s_in


def finish_kernel(seq_len, leads, masks, count, queries, *refs):
    blocks, scores = refs[:-1], refs[-1]
    rank = blocks[0].shape[1] // 2

    @pl.when(leads())
    def _():
        pairs = [ref[:rank] for ref in blocks]
        total = [ref[rank:] for ref in blocks[:count]]
        while len(total) > 1:
            total = [total[n] + total[n + 1] for n in range(0, len(total), 2)]
        left, inv_in, c_out, c_in = solve(rank, total[0], pairs[masks.index(0)])
        left = left * c_out
        zero = jnp.zeros((rank, rank), jnp.float32)
        right = jnp.concatenate(
            [jnp.concatenate([inv_in, zero], axis=1), jnp.concatenate([zero, inv_in], axis=1)], axis=0
        )
        straight = dot_hi(left, right) * c_in
        crossed = pltpu.roll(straight, rank, 1)
        size = len(pairs)
        sums = [jnp.sum(pair * straight, axis=0, keepdims=True) for pair in pairs]
        sums += [jnp.sum(pair * crossed, axis=0, keepdims=True) for pair in pairs]
        sums = jnp.concatenate(sums, axis=0)
        num = queries.shape[1]
        index = lax.broadcasted_iota(jnp.int32, (2 * size, num), 0) % size
        mask = sum(jnp.where(index == n, value, 0) for n, value in enumerate(masks))
        device = lax.axis_index("dp") ^ mask
        chosen = queries[...]
        second = jnp.where(chosen == 2 * device + 1, jnp.sum(sums[:, :rank], axis=1, keepdims=True), 0.0)
        first = jnp.where(chosen == 2 * device, jnp.sum(sums[:, rank:], axis=1, keepdims=True), 0.0)
        scale = 1.0 / (rank * seq_len)
        scores[0:1, :] = scale * jnp.sum(
            jnp.concatenate([first[:size], second[size:]], axis=0), axis=0, keepdims=True
        )
        scores[1:2, :] = scale * jnp.sum(
            jnp.concatenate([second[:size], first[size:]], axis=0), axis=0, keepdims=True
        )


def publish_kernel(scores, out, sem):
    copy = pltpu.make_async_copy(scores, out, sem)
    copy.start()
    copy.wait()


def replace_kernel(leads, theirs, mine, out, sem):
    @pl.when(jnp.logical_not(leads()))
    def _():
        copy = pltpu.make_async_copy(theirs, out, sem)
        copy.start()
        copy.wait()


def shape(*dims):
    return pltpu.VMEM(dims, jnp.float32)


def call(kernel, name, out_shape, *operands):
    return pl.pallas_call(
        kernel,
        out_shape=out_shape,
        in_specs=[VMEM] * len(operands),
        out_specs=VMEM,
        compiler_params=pltpu.CompilerParams(vmem_limit_bytes=4 * 2**20),
        name=name,
    )(*[pltpu.with_memory_space_constraint(operand, pltpu.VMEM) for operand in operands])


def project(activations, out_grads, proj_in, proj_out, lengths):
    examples, seq_len, hidden = activations.shape
    rank = proj_in.shape[0]
    stages = 3 if hidden % 256 == 0 else 2
    operands = [lengths, activations, out_grads, proj_in, proj_out]
    return pl.pallas_call(
        project_kernel,
        out_shape=[shape(examples * seq_len, 2 * rank), shape(8, 2 * rank)],
        in_specs=[HBM] * 5,
        out_specs=[VMEM] * 2,
        scratch_shapes=[pltpu.SMEM(lengths.shape, jnp.int32)]
        + [pltpu.VMEM(operand.shape, jnp.bfloat16) for operand in operands[1:]]
        + [pltpu.VMEM((examples * seq_len, rank), jnp.float32)] * 2
        + [pltpu.SemaphoreType.DMA((2 * stages + 2,))],
        compiler_params=pltpu.CompilerParams(vmem_limit_bytes=24 * 2**20),
        name="project",
    )(*[pltpu.with_memory_space_constraint(operand, pltpu.HBM) for operand in operands])


def swap(x, dp, tensor, far, near):
    pairs = []
    for d in range(dp):
        for t in range(tensor):
            masks = far if t % 2 else near
            pairs.append((d * tensor + t, (d ^ masks[0]) * tensor + (t ^ masks[1])))
    return lax.ppermute(x, ("dp", "tensor"), pairs)


def across(x, tensor):
    return lax.ppermute(x, "tensor", [(t, t ^ 1) for t in range(tensor)])


def publish(scores):
    return pl.pallas_call(
        publish_kernel,
        out_shape=jax.ShapeDtypeStruct(scores.shape, scores.dtype),
        in_specs=[VMEM],
        out_specs=HBM,
        scratch_shapes=[pltpu.SemaphoreType.DMA],
        compiler_params=pltpu.CompilerParams(vmem_limit_bytes=2**20),
        cost_estimate=pl.CostEstimate(flops=10**9, bytes_accessed=0, transcendentals=0),
        name="publish",
    )(pltpu.with_memory_space_constraint(scores, pltpu.VMEM))


def replace(theirs, mine, leads):
    return pl.pallas_call(
        functools.partial(replace_kernel, leads),
        out_shape=jax.ShapeDtypeStruct(mine.shape, mine.dtype),
        in_specs=[VMEM, HBM],
        out_specs=HBM,
        scratch_shapes=[pltpu.SemaphoreType.DMA],
        input_output_aliases={1: 0},
        compiler_params=pltpu.CompilerParams(vmem_limit_bytes=2**20),
        name="replace",
    )(pltpu.with_memory_space_constraint(theirs, pltpu.VMEM), mine)


def per_device(dp, tensor, activations, out_grads, proj_in, proj_out, lengths, query_ids):
    examples, seq_len, _ = activations.shape
    rank = proj_in.shape[1]
    num = query_ids.shape[0]
    paired = dp == 4 and tensor == 4
    odd = lambda: lax.rem(lax.axis_index("tensor"), 2) == 1
    leads = odd if paired else lambda: True
    sketch, live = project(activations, out_grads, proj_in.T, proj_out.T, lengths)
    sketch = sketch + across(sketch, tensor)
    if paired:
        other = swap(sketch, dp, tensor, (0, 2), (1, 0))
    else:
        other = jnp.zeros_like(sketch)
        step = 2
        while step < tensor:
            sketch = sketch + lax.ppermute(sketch, "tensor", [(t, t ^ step) for t in range(tensor)])
            step *= 2
    packed = call(
        functools.partial(gram_kernel, seq_len, leads),
        "gram",
        shape(rank + rank // 2 + 8, 2 * rank),
        live,
        sketch,
        other,
    )
    if paired:
        own = packed
        near = swap(packed, dp, tensor, (1, 0), (0, 2))
        other = swap(packed, dp, tensor, (2, 0), (0, 2))
        merged = call(
            functools.partial(merge_kernel, leads), "merge", shape(rank + rank // 2 + 8, 2 * rank), packed, other
        )
        blocks = [merged, swap(merged, dp, tensor, (1, 0), (0, 2)), own, near]
        masks = [2, 3, 0, 1]
        count = 2
    else:
        masks = list(range(dp))
        count = dp
        order = lax.axis_index("dp") ^ jnp.arange(dp, dtype=jnp.int32)
        gathered = lax.all_gather(packed, "dp", axis=0)[order]
        blocks = [gathered[n] for n in range(dp)]
    scores = call(
        functools.partial(finish_kernel, seq_len, leads, masks, count),
        "finish",
        shape(examples, num),
        query_ids.reshape(1, num),
        *blocks,
    )
    if paired:
        other = across(scores, tensor)
        scores = replace(other, publish(scores), leads)
    return scores.T


def solution(mesh):
    placed = (
        P(("groups", "dp"), None, "tensor"),
        P(("groups", "dp"), None, "tensor"),
        P("tensor", None),
        P("tensor", None),
        P(("groups", "dp")),
        P("groups"),
    )
    return jax.shard_map(
        functools.partial(per_device, mesh.shape["dp"], mesh.shape["tensor"]),
        mesh=mesh,
        in_specs=placed,
        out_specs=P(None, ("groups", "dp")),
        check_vma=False,
    )
```

```python
import functools

import jax
import jax.numpy as jnp
from jax import lax
from jax.experimental import pallas as pl
from jax.experimental.pallas import tpu as pltpu
from jax.sharding import PartitionSpec as P

HIGH = lax.Precision.HIGHEST
VMEM = pl.BlockSpec(memory_space=pltpu.VMEM)
HBM = pl.BlockSpec(memory_space=pltpu.HBM)
DAMP = 0.1
STEPS = 5


def dot_nt(a, b):
    return lax.dot_general(a, b, (((1,), (1,)), ((), ())), preferred_element_type=jnp.float32)


def dot_hi(a, b):
    return jnp.dot(a, b, precision=HIGH, preferred_element_type=jnp.float32)


def project_kernel(lengths, act, grad, proj_in, proj_out, sketch, live, len_s, act_v, grad_v, pin_v, pout_v, out_v, in_v, sems):
    examples, seq_len, hidden = act.shape
    rank = proj_in.shape[0]
    tokens = examples * seq_len
    stages = sems.shape[0] // 2 - 1
    width = hidden // (stages - 1)
    copies = []

    def begin(src, dst):
        copy = pltpu.make_async_copy(src, dst, sems.at[len(copies)])
        copy.start()
        copies.append(copy)

    begin(proj_out, pout_v)
    begin(grad, grad_v)
    for n in range(stages - 1):
        span = pl.ds(n * width, width)
        begin(proj_in.at[:, span], pin_v.at[:, span])
        begin(act.at[:, :, span], act_v.at[:, :, span])
    begin(lengths, len_s)

    def stage(n):
        copies[2 * n].wait()
        copies[2 * n + 1].wait()
        if n == 0:
            out_v[...] = dot_nt(grad_v[...].reshape(tokens, -1), pout_v[...])
            return
        span = pl.ds((n - 1) * width, width)
        in_part = dot_nt(act_v[:, :, span].reshape(tokens, width), pin_v[:, span])
        if n > 1:
            in_part += in_v[...]
        if n < stages - 1:
            in_v[...] = in_part
            return
        both = jnp.concatenate([out_v[...], in_part], axis=1)
        token = lax.broadcasted_iota(jnp.int32, (seq_len, 2 * rank), 0)
        copies[-1].wait()
        count = jnp.int32(0)
        for e in range(examples):
            rows = pl.ds(e * seq_len, seq_len)
            sketch[rows] = jnp.where(token < len_s[e], both[e * seq_len : (e + 1) * seq_len], 0.0)
            count += len_s[e]
        live[...] = jnp.full(live.shape, count.astype(jnp.float32))

    @pl.loop(0, stages)
    def _(turn):
        for n in range(stages):
            pl.when(turn == n)(functools.partial(stage, n))


def gram_kernel(seq_len, leads, live, mine, theirs, packed):
    rank = mine.shape[1] // 2
    half = rank // 2

    @pl.when(leads())
    def _():
        tokens = mine[...] + theirs[...]
        grams = []
        for e in range(2):
            block = tokens[e * seq_len : (e + 1) * seq_len]
            grams.append(
                lax.dot_general(
                    block, block, (((0,), (0,)), ((), ())), precision=HIGH, preferred_element_type=jnp.float32
                )
            )
        total = grams[0] + grams[1]
        high, low = total[:rank], total[rank:]
        row = lax.broadcasted_iota(jnp.int32, (half, 2 * rank), 0)
        lane = lax.broadcasted_iota(jnp.int32, (half, 2 * rank), 1)
        packed[rank : rank + half] = jnp.where(
            lane < rank,
            jnp.where(lane <= row, high[:half], pltpu.roll(low[:half], rank, 1)),
            jnp.where(lane - rank <= row + half, pltpu.roll(high[half:], rank, 1), low[half:]),
        )
        row = lax.broadcasted_iota(jnp.int32, (rank, 2 * rank), 0)
        lane = lax.broadcasted_iota(jnp.int32, (rank, 2 * rank), 1)
        diag_in = jnp.sum(jnp.where(lane == rank + row, low, 0.0), axis=0, keepdims=True)
        diag_out = jnp.sum(jnp.where(lane == row, high, 0.0), axis=0, keepdims=True)
        tail = jnp.where(row[:8] == 1, live[...], diag_in + diag_out)
        packed[rank + half :] = tail
        packed[:rank] = jnp.where(lane < rank, pltpu.roll(grams[1][:rank], rank, 1), grams[0][:rank])


def merge_kernel(leads, mine, theirs, merged):
    rank = mine.shape[1] // 2

    @pl.when(leads())
    def _():
        merged[:rank] = theirs[:rank]
        merged[rank:] = mine[rank:] + theirs[rank:]


def normalised(rank, total):
    half = rank // 2
    mixed = jnp.concatenate([total[:half, :rank], total[:half, rank:]], axis=0)
    turned = mixed.T
    diag = total[half : half + 1, rank:]
    diags = total[half : half + 1]
    count = total[half + 1 : half + 2, :1]
    row = lax.broadcasted_iota(jnp.int32, (rank, rank), 0)
    lane = lax.broadcasted_iota(jnp.int32, (rank, rank), 1)
    eye = row == lane
    sum_out = jnp.where(lane <= row, mixed, turned)
    sum_in = jnp.where(lane > row, mixed, jnp.where(eye, diag, turned))

    def divide(sums, diag):
        inverse = 1.0 / jnp.sum(diag, axis=1, keepdims=True)
        return sums * inverse + jnp.where(eye, DAMP / rank, 0.0), count * inverse

    return *divide(sum_out, diags[:, :rank]), *divide(sum_in, diags[:, rank:]), jnp.where(eye, 1.0, 0.0)


def total_square(matrix):
    return jnp.sum(jnp.sum(matrix * matrix, axis=0, keepdims=True), axis=1, keepdims=True)


def solve(rank, total, right):
    d_out, c_out, d_in, c_in, eye = normalised(rank, total)

    def scale(matrix):
        mean = (1.0 + DAMP) / rank
        spread = jnp.sqrt(jnp.maximum(total_square(matrix) / rank - mean * mean, 0.0))
        return 2.0 / (mean + spread * (rank - 1) ** 0.5 + DAMP / rank)

    s_out, s_in = scale(d_out), scale(d_in)
    t_out = s_out * (2.0 * d_out - s_out * dot_hi(d_out, d_out))
    t_in = s_in * (2.0 * d_in - s_in * dot_hi(d_in, d_in))
    right = 2.0 * right - s_out * dot_hi(d_out, right)
    x_in = 2.0 * eye - s_in * d_in

    def square(t_out, t_in):
        return 2.0 * t_out - dot_hi(t_out, t_out), 2.0 * t_in - dot_hi(t_in, t_in)

    def update(t_out, t_in, right, x_in):
        return 2.0 * right - dot_hi(t_out, right), 2.0 * x_in - dot_hi(x_in, t_in)

    def residual(t_out, t_in):
        return jnp.sum(jnp.maximum(total_square(eye - t_out), total_square(eye - t_in)))

    for n in range(STEPS - 1):
        right, x_in = update(t_out, t_in, right, x_in)
        if n < STEPS - 2:
            t_out, t_in = square(t_out, t_in)

    def unfinished(state):
        return jnp.logical_and(state[0] > 3e-5, state[1] < 40)

    def more(state):
        _, n, t_out, t_in, right, x_in = state
        t_out, t_in = square(t_out, t_in)
        right, x_in = update(t_out, t_in, right, x_in)
        return residual(t_out, t_in), n + 1, t_out, t_in, right, x_in

    state = (residual(t_out, t_in), jnp.int32(0), t_out, t_in, right, x_in)
    _, _, _, _, right, x_in = lax.while_loop(unfinished, more, state)
    return right, x_in, c_out * s_out, c_in * s_in


def finish_kernel(seq_len, leads, masks, count, queries, *refs):
    blocks, scores = refs[:-1], refs[-1]
    rank = blocks[0].shape[1] // 2

    @pl.when(leads())
    def _():
        pairs = [ref[:rank] for ref in blocks]
        total = [ref[rank:] for ref in blocks[:count]]
        while len(total) > 1:
            total = [total[n] + total[n + 1] for n in range(0, len(total), 2)]
        left, inv_in, c_out, c_in = solve(rank, total[0], pairs[masks.index(0)])
        left = left * c_out
        zero = jnp.zeros((rank, rank), jnp.float32)
        right = jnp.concatenate(
            [jnp.concatenate([inv_in, zero], axis=1), jnp.concatenate([zero, inv_in], axis=1)], axis=0
        )
        straight = dot_hi(left, right) * c_in
        crossed = pltpu.roll(straight, rank, 1)
        size = len(pairs)
        sums = [jnp.sum(pair * straight, axis=0, keepdims=True) for pair in pairs]
        sums += [jnp.sum(pair * crossed, axis=0, keepdims=True) for pair in pairs]
        sums = jnp.concatenate(sums, axis=0)
        num = queries.shape[1]
        index = lax.broadcasted_iota(jnp.int32, (2 * size, num), 0) % size
        mask = sum(jnp.where(index == n, value, 0) for n, value in enumerate(masks))
        device = lax.axis_index("dp") ^ mask
        chosen = queries[...]
        second = jnp.where(chosen == 2 * device + 1, jnp.sum(sums[:, :rank], axis=1, keepdims=True), 0.0)
        first = jnp.where(chosen == 2 * device, jnp.sum(sums[:, rank:], axis=1, keepdims=True), 0.0)
        scale = 1.0 / (rank * seq_len)
        scores[0:1, :] = scale * jnp.sum(
            jnp.concatenate([first[:size], second[size:]], axis=0), axis=0, keepdims=True
        )
        scores[1:2, :] = scale * jnp.sum(
            jnp.concatenate([second[:size], first[size:]], axis=0), axis=0, keepdims=True
        )


def publish_kernel(scores, out, sem):
    copy = pltpu.make_async_copy(scores, out, sem)
    copy.start()
    copy.wait()


def replace_kernel(leads, theirs, mine, out, sem):
    @pl.when(jnp.logical_not(leads()))
    def _():
        copy = pltpu.make_async_copy(theirs, out, sem)
        copy.start()
        copy.wait()


def shape(*dims):
    return pltpu.VMEM(dims, jnp.float32)


def call(kernel, name, out_shape, *operands):
    return pl.pallas_call(
        kernel,
        out_shape=out_shape,
        in_specs=[VMEM] * len(operands),
        out_specs=VMEM,
        compiler_params=pltpu.CompilerParams(vmem_limit_bytes=4 * 2**20),
        name=name,
    )(*[pltpu.with_memory_space_constraint(operand, pltpu.VMEM) for operand in operands])


def project(activations, out_grads, proj_in, proj_out, lengths):
    examples, seq_len, hidden = activations.shape
    rank = proj_in.shape[0]
    stages = 3 if hidden % 256 == 0 else 2
    operands = [lengths, activations, out_grads, proj_in, proj_out]
    return pl.pallas_call(
        project_kernel,
        out_shape=[shape(examples * seq_len, 2 * rank), shape(8, 2 * rank)],
        in_specs=[HBM] * 5,
        out_specs=[VMEM] * 2,
        scratch_shapes=[pltpu.SMEM(lengths.shape, jnp.int32)]
        + [pltpu.VMEM(operand.shape, jnp.bfloat16) for operand in operands[1:]]
        + [pltpu.VMEM((examples * seq_len, rank), jnp.float32)] * 2
        + [pltpu.SemaphoreType.DMA((2 * stages + 2,))],
        compiler_params=pltpu.CompilerParams(vmem_limit_bytes=24 * 2**20),
        name="project",
    )(*[pltpu.with_memory_space_constraint(operand, pltpu.HBM) for operand in operands])


def swap(x, dp, tensor, far, near):
    pairs = []
    for d in range(dp):
        for t in range(tensor):
            masks = far if t % 2 else near
            pairs.append((d * tensor + t, (d ^ masks[0]) * tensor + (t ^ masks[1])))
    return lax.ppermute(x, ("dp", "tensor"), pairs)


def across(x, tensor):
    return lax.ppermute(x, "tensor", [(t, t ^ 1) for t in range(tensor)])


def publish(scores):
    return pl.pallas_call(
        publish_kernel,
        out_shape=jax.ShapeDtypeStruct(scores.shape, scores.dtype),
        in_specs=[VMEM],
        out_specs=HBM,
        scratch_shapes=[pltpu.SemaphoreType.DMA],
        compiler_params=pltpu.CompilerParams(vmem_limit_bytes=2**20),
        cost_estimate=pl.CostEstimate(flops=10**9, bytes_accessed=0, transcendentals=0),
        name="publish",
    )(pltpu.with_memory_space_constraint(scores, pltpu.VMEM))


def replace(theirs, mine, leads):
    return pl.pallas_call(
        functools.partial(replace_kernel, leads),
        out_shape=jax.ShapeDtypeStruct(mine.shape, mine.dtype),
        in_specs=[VMEM, HBM],
        out_specs=HBM,
        scratch_shapes=[pltpu.SemaphoreType.DMA],
        input_output_aliases={1: 0},
        compiler_params=pltpu.CompilerParams(vmem_limit_bytes=2**20),
        name="replace",
    )(pltpu.with_memory_space_constraint(theirs, pltpu.VMEM), mine)


def per_device(dp, tensor, activations, out_grads, proj_in, proj_out, lengths, query_ids):
    examples, seq_len, _ = activations.shape
    rank = proj_in.shape[1]
    num = query_ids.shape[0]
    paired = dp == 4 and tensor == 4
    odd = lambda: lax.rem(lax.axis_index("tensor"), 2) == 1
    leads = odd if paired else lambda: True
    sketch, live = project(activations, out_grads, proj_in.T, proj_out.T, lengths)
    sketch = sketch + across(sketch, tensor)
    if paired:
        other = swap(sketch, dp, tensor, (0, 2), (1, 0))
    else:
        other = jnp.zeros_like(sketch)
        step = 2
        while step < tensor:
            sketch = sketch + lax.ppermute(sketch, "tensor", [(t, t ^ step) for t in range(tensor)])
            step *= 2
    packed = call(
        functools.partial(gram_kernel, seq_len, leads),
        "gram",
        shape(rank + rank // 2 + 8, 2 * rank),
        live,
        sketch,
        other,
    )
    if paired:
        own = packed
        near = swap(packed, dp, tensor, (1, 0), (0, 2))
        other = swap(packed, dp, tensor, (2, 0), (0, 2))
        merged = call(
            functools.partial(merge_kernel, leads), "merge", shape(rank + rank // 2 + 8, 2 * rank), packed, other
        )
        blocks = [merged, swap(merged, dp, tensor, (1, 0), (0, 2)), own, near]
        masks = [2, 3, 0, 1]
        count = 2
    else:
        masks = list(range(dp))
        count = dp
        order = lax.axis_index("dp") ^ jnp.arange(dp, dtype=jnp.int32)
        gathered = lax.all_gather(packed, "dp", axis=0)[order]
        blocks = [gathered[n] for n in range(dp)]
    scores = call(
        functools.partial(finish_kernel, seq_len, leads, masks, count),
        "finish",
        shape(examples, num),
        query_ids.reshape(1, num),
        *blocks,
    )
    if paired:
        other = across(scores, tensor)
        scores = replace(other, publish(scores), leads)
    return scores.T


def solution(mesh):
    placed = (
        P(("groups", "dp"), None, "tensor"),
        P(("groups", "dp"), None, "tensor"),
        P("tensor", None),
        P("tensor", None),
        P(("groups", "dp")),
        P("groups"),
    )
    return jax.shard_map(
        functools.partial(per_device, mesh.shape["dp"], mesh.shape["tensor"]),
        mesh=mesh,
        in_specs=placed,
        out_specs=P(None, ("groups", "dp")),
        check_vma=False,
    )
```

```python
import functools

import jax
import jax.numpy as jnp
from jax import lax
from jax.experimental import pallas as pl
from jax.experimental.pallas import tpu as pltpu
from jax.sharding import PartitionSpec as P

HIGH = lax.Precision.HIGHEST
VMEM = pl.BlockSpec(memory_space=pltpu.VMEM)
HBM = pl.BlockSpec(memory_space=pltpu.HBM)
DAMP = 0.1
STEPS = 5


def dot_nt(a, b):
    return lax.dot_general(a, b, (((1,), (1,)), ((), ())), preferred_element_type=jnp.float32)


def dot_hi(a, b):
    return jnp.dot(a, b, precision=HIGH, preferred_element_type=jnp.float32)


def project_kernel(lengths, act, grad, proj_in, proj_out, sketch, live, len_s, act_v, grad_v, pin_v, pout_v, out_v, in_v, sems):
    examples, seq_len, hidden = act.shape
    rank = proj_in.shape[0]
    tokens = examples * seq_len
    stages = sems.shape[0] // 2 - 1
    width = hidden // (stages - 1)
    copies = []

    def begin(src, dst):
        copy = pltpu.make_async_copy(src, dst, sems.at[len(copies)])
        copy.start()
        copies.append(copy)

    begin(proj_out, pout_v)
    begin(grad, grad_v)
    for n in range(stages - 1):
        span = pl.ds(n * width, width)
        begin(proj_in.at[:, span], pin_v.at[:, span])
        begin(act.at[:, :, span], act_v.at[:, :, span])
    begin(lengths, len_s)

    def stage(n):
        copies[2 * n].wait()
        copies[2 * n + 1].wait()
        if n == 0:
            out_v[...] = dot_nt(grad_v[...].reshape(tokens, -1), pout_v[...])
            return
        span = pl.ds((n - 1) * width, width)
        in_part = dot_nt(act_v[:, :, span].reshape(tokens, width), pin_v[:, span])
        if n > 1:
            in_part += in_v[...]
        if n < stages - 1:
            in_v[...] = in_part
            return
        both = jnp.concatenate([out_v[...], in_part], axis=1)
        token = lax.broadcasted_iota(jnp.int32, (seq_len, 2 * rank), 0)
        copies[-1].wait()
        count = jnp.int32(0)
        for e in range(examples):
            rows = pl.ds(e * seq_len, seq_len)
            sketch[rows] = jnp.where(token < len_s[e], both[e * seq_len : (e + 1) * seq_len], 0.0)
            count += len_s[e]
        live[...] = jnp.full(live.shape, count.astype(jnp.float32))

    @pl.loop(0, stages)
    def _(turn):
        for n in range(stages):
            pl.when(turn == n)(functools.partial(stage, n))


def gram_kernel(seq_len, leads, live, mine, theirs, packed):
    rank = mine.shape[1] // 2
    half = rank // 2

    @pl.when(leads())
    def _():
        tokens = mine[...] + theirs[...]
        grams = []
        for e in range(2):
            block = tokens[e * seq_len : (e + 1) * seq_len]
            grams.append(
                lax.dot_general(
                    block, block, (((0,), (0,)), ((), ())), precision=HIGH, preferred_element_type=jnp.float32
                )
            )
        total = grams[0] + grams[1]
        high, low = total[:rank], total[rank:]
        row = lax.broadcasted_iota(jnp.int32, (half, 2 * rank), 0)
        lane = lax.broadcasted_iota(jnp.int32, (half, 2 * rank), 1)
        packed[rank : rank + half] = jnp.where(
            lane < rank,
            jnp.where(lane <= row, high[:half], pltpu.roll(low[:half], rank, 1)),
            jnp.where(lane - rank <= row + half, pltpu.roll(high[half:], rank, 1), low[half:]),
        )
        row = lax.broadcasted_iota(jnp.int32, (rank, 2 * rank), 0)
        lane = lax.broadcasted_iota(jnp.int32, (rank, 2 * rank), 1)
        diag_in = jnp.sum(jnp.where(lane == rank + row, low, 0.0), axis=0, keepdims=True)
        diag_out = jnp.sum(jnp.where(lane == row, high, 0.0), axis=0, keepdims=True)
        tail = jnp.where(row[:8] == 1, live[...], diag_in + diag_out)
        packed[rank + half :] = tail
        packed[:rank] = jnp.where(lane < rank, pltpu.roll(grams[1][:rank], rank, 1), grams[0][:rank])


def merge_kernel(leads, mine, theirs, merged):
    rank = mine.shape[1] // 2

    @pl.when(leads())
    def _():
        merged[:rank] = theirs[:rank]
        merged[rank:] = mine[rank:] + theirs[rank:]


def normalised(rank, total):
    half = rank // 2
    mixed = jnp.concatenate([total[:half, :rank], total[:half, rank:]], axis=0)
    turned = mixed.T
    diag = total[half : half + 1, rank:]
    diags = total[half : half + 1]
    count = total[half + 1 : half + 2, :1]
    row = lax.broadcasted_iota(jnp.int32, (rank, rank), 0)
    lane = lax.broadcasted_iota(jnp.int32, (rank, rank), 1)
    eye = row == lane
    sum_out = jnp.where(lane <= row, mixed, turned)
    sum_in = jnp.where(lane > row, mixed, jnp.where(eye, diag, turned))

    def divide(sums, diag):
        inverse = 1.0 / jnp.sum(diag, axis=1, keepdims=True)
        return sums * inverse + jnp.where(eye, DAMP / rank, 0.0), count * inverse

    return *divide(sum_out, diags[:, :rank]), *divide(sum_in, diags[:, rank:]), jnp.where(eye, 1.0, 0.0)


def total_square(matrix):
    return jnp.sum(jnp.sum(matrix * matrix, axis=0, keepdims=True), axis=1, keepdims=True)


def solve(rank, total, right):
    d_out, c_out, d_in, c_in, eye = normalised(rank, total)

    def scale(matrix):
        mean = (1.0 + DAMP) / rank
        spread = jnp.sqrt(jnp.maximum(total_square(matrix) / rank - mean * mean, 0.0))
        return 2.0 / (mean + spread * (rank - 1) ** 0.5 + DAMP / rank)

    s_out, s_in = scale(d_out), scale(d_in)
    t_out = s_out * (2.0 * d_out - s_out * dot_hi(d_out, d_out))
    t_in = s_in * (2.0 * d_in - s_in * dot_hi(d_in, d_in))
    right = 2.0 * right - s_out * dot_hi(d_out, right)
    x_in = 2.0 * eye - s_in * d_in

    def square(t_out, t_in):
        return 2.0 * t_out - dot_hi(t_out, t_out), 2.0 * t_in - dot_hi(t_in, t_in)

    def update(t_out, t_in, right, x_in):
        return 2.0 * right - dot_hi(t_out, right), 2.0 * x_in - dot_hi(x_in, t_in)

    def residual(t_out, t_in):
        return jnp.sum(jnp.maximum(total_square(eye - t_out), total_square(eye - t_in)))

    for n in range(STEPS - 1):
        right, x_in = update(t_out, t_in, right, x_in)
        if n < STEPS - 2:
            t_out, t_in = square(t_out, t_in)

    def unfinished(state):
        return jnp.logical_and(state[0] > 3e-5, state[1] < 40)

    def more(state):
        _, n, t_out, t_in, right, x_in = state
        t_out, t_in = square(t_out, t_in)
        right, x_in = update(t_out, t_in, right, x_in)
        return residual(t_out, t_in), n + 1, t_out, t_in, right, x_in

    state = (residual(t_out, t_in), jnp.int32(0), t_out, t_in, right, x_in)
    _, _, _, _, right, x_in = lax.while_loop(unfinished, more, state)
    return right, x_in, c_out * s_out, c_in * s_in


def finish_kernel(seq_len, leads, masks, count, queries, *refs):
    blocks, scores = refs[:-1], refs[-1]
    rank = blocks[0].shape[1] // 2

    @pl.when(leads())
    def _():
        pairs = [ref[:rank] for ref in blocks]
        total = [ref[rank:] for ref in blocks[:count]]
        while len(total) > 1:
            total = [total[n] + total[n + 1] for n in range(0, len(total), 2)]
        left, inv_in, c_out, c_in = solve(rank, total[0], pairs[masks.index(0)])
        left = left * c_out
        zero = jnp.zeros((rank, rank), jnp.float32)
        beside = jnp.concatenate([inv_in, zero, zero, inv_in], axis=1)
        before = jnp.concatenate([zero, inv_in, inv_in, zero], axis=1)
        both = dot_hi(left, jnp.concatenate([beside, before], axis=0)) * c_in
        straight, crossed = both[:, : 2 * rank], both[:, 2 * rank :]
        size = len(pairs)
        sums = [jnp.sum(pair * straight, axis=0, keepdims=True) for pair in pairs]
        sums += [jnp.sum(pair * crossed, axis=0, keepdims=True) for pair in pairs]
        sums = jnp.concatenate(sums, axis=0)
        inner = lax.broadcasted_iota(jnp.int32, sums.shape, 1) < rank
        second = jnp.sum(jnp.where(inner, sums, 0.0), axis=1, keepdims=True)
        first = jnp.sum(jnp.where(inner, 0.0, sums), axis=1, keepdims=True)
        row = lax.broadcasted_iota(jnp.int32, (2 * size, queries.shape[1]), 0)
        mask = sum(jnp.where(row % size == n, value, 0) for n, value in enumerate(masks))
        example = 2 * (lax.axis_index("dp") ^ mask)
        chosen = queries[...]
        scale = 1.0 / (rank * seq_len)
        second = jnp.where(chosen == example + 1, scale * second, 0.0)
        first = jnp.where(chosen == example, scale * first, 0.0)
        same = row < size
        scores[0:1, :] = jnp.sum(jnp.where(same, first, second), axis=0, keepdims=True)
        scores[1:2, :] = jnp.sum(jnp.where(same, second, first), axis=0, keepdims=True)


def publish_kernel(scores, out, sem):
    copy = pltpu.make_async_copy(scores, out, sem)
    copy.start()
    copy.wait()


def replace_kernel(leads, theirs, mine, out, sem):
    @pl.when(jnp.logical_not(leads()))
    def _():
        copy = pltpu.make_async_copy(theirs, out, sem)
        copy.start()
        copy.wait()


def shape(*dims):
    return pltpu.VMEM(dims, jnp.float32)


def call(kernel, name, out_shape, *operands):
    return pl.pallas_call(
        kernel,
        out_shape=out_shape,
        in_specs=[VMEM] * len(operands),
        out_specs=VMEM,
        compiler_params=pltpu.CompilerParams(vmem_limit_bytes=4 * 2**20),
        name=name,
    )(*[pltpu.with_memory_space_constraint(operand, pltpu.VMEM) for operand in operands])


def project(activations, out_grads, proj_in, proj_out, lengths):
    examples, seq_len, hidden = activations.shape
    rank = proj_in.shape[0]
    stages = 3 if hidden % 256 == 0 else 2
    operands = [lengths, activations, out_grads, proj_in, proj_out]
    return pl.pallas_call(
        project_kernel,
        out_shape=[shape(examples * seq_len, 2 * rank), shape(8, 2 * rank)],
        in_specs=[HBM] * 5,
        out_specs=[VMEM] * 2,
        scratch_shapes=[pltpu.SMEM(lengths.shape, jnp.int32)]
        + [pltpu.VMEM(operand.shape, jnp.bfloat16) for operand in operands[1:]]
        + [pltpu.VMEM((examples * seq_len, rank), jnp.float32)] * 2
        + [pltpu.SemaphoreType.DMA((2 * stages + 2,))],
        compiler_params=pltpu.CompilerParams(vmem_limit_bytes=24 * 2**20),
        name="project",
    )(*[pltpu.with_memory_space_constraint(operand, pltpu.HBM) for operand in operands])


def swap(x, dp, tensor, far, near):
    pairs = []
    for d in range(dp):
        for t in range(tensor):
            masks = far if t % 2 else near
            pairs.append((d * tensor + t, (d ^ masks[0]) * tensor + (t ^ masks[1])))
    return lax.ppermute(x, ("dp", "tensor"), pairs)


def across(x, tensor):
    return lax.ppermute(x, "tensor", [(t, t ^ 1) for t in range(tensor)])


def publish(scores):
    return pl.pallas_call(
        publish_kernel,
        out_shape=jax.ShapeDtypeStruct(scores.shape, scores.dtype),
        in_specs=[VMEM],
        out_specs=HBM,
        scratch_shapes=[pltpu.SemaphoreType.DMA],
        compiler_params=pltpu.CompilerParams(vmem_limit_bytes=2**20),
        cost_estimate=pl.CostEstimate(flops=10**9, bytes_accessed=0, transcendentals=0),
        name="publish",
    )(pltpu.with_memory_space_constraint(scores, pltpu.VMEM))


def replace(theirs, mine, leads):
    return pl.pallas_call(
        functools.partial(replace_kernel, leads),
        out_shape=jax.ShapeDtypeStruct(mine.shape, mine.dtype),
        in_specs=[VMEM, HBM],
        out_specs=HBM,
        scratch_shapes=[pltpu.SemaphoreType.DMA],
        input_output_aliases={1: 0},
        compiler_params=pltpu.CompilerParams(vmem_limit_bytes=2**20),
        name="replace",
    )(pltpu.with_memory_space_constraint(theirs, pltpu.VMEM), mine)


def per_device(dp, tensor, activations, out_grads, proj_in, proj_out, lengths, query_ids):
    examples, seq_len, _ = activations.shape
    rank = proj_in.shape[1]
    num = query_ids.shape[0]
    paired = dp == 4 and tensor == 4
    odd = lambda: lax.rem(lax.axis_index("tensor"), 2) == 1
    leads = odd if paired else lambda: True
    sketch, live = project(activations, out_grads, proj_in.T, proj_out.T, lengths)
    sketch = sketch + across(sketch, tensor)
    if paired:
        other = swap(sketch, dp, tensor, (0, 2), (1, 0))
    else:
        other = jnp.zeros_like(sketch)
        step = 2
        while step < tensor:
            sketch = sketch + lax.ppermute(sketch, "tensor", [(t, t ^ step) for t in range(tensor)])
            step *= 2
    packed = call(
        functools.partial(gram_kernel, seq_len, leads),
        "gram",
        shape(rank + rank // 2 + 8, 2 * rank),
        live,
        sketch,
        other,
    )
    if paired:
        own = packed
        near = swap(packed, dp, tensor, (1, 0), (0, 2))
        other = swap(packed, dp, tensor, (2, 0), (0, 2))
        merged = call(
            functools.partial(merge_kernel, leads), "merge", shape(rank + rank // 2 + 8, 2 * rank), packed, other
        )
        blocks = [merged, swap(merged, dp, tensor, (1, 0), (0, 2)), own, near]
        masks = [2, 3, 0, 1]
        count = 2
    else:
        masks = list(range(dp))
        count = dp
        order = lax.axis_index("dp") ^ jnp.arange(dp, dtype=jnp.int32)
        gathered = lax.all_gather(packed, "dp", axis=0)[order]
        blocks = [gathered[n] for n in range(dp)]
    scores = call(
        functools.partial(finish_kernel, seq_len, leads, masks, count),
        "finish",
        shape(examples, num),
        query_ids.reshape(1, num),
        *blocks,
    )
    if paired:
        other = across(scores, tensor)
        scores = replace(other, publish(scores), leads)
    return scores.T


def solution(mesh):
    placed = (
        P(("groups", "dp"), None, "tensor"),
        P(("groups", "dp"), None, "tensor"),
        P("tensor", None),
        P("tensor", None),
        P(("groups", "dp")),
        P("groups"),
    )
    return jax.shard_map(
        functools.partial(per_device, mesh.shape["dp"], mesh.shape["tensor"]),
        mesh=mesh,
        in_specs=placed,
        out_specs=P(None, ("groups", "dp")),
        check_vma=False,
    )
```

```python
import functools

import jax
import jax.numpy as jnp
from jax import lax
from jax.experimental import pallas as pl
from jax.experimental.pallas import tpu as pltpu
from jax.sharding import PartitionSpec as P

HIGH = lax.Precision.HIGHEST
VMEM = pl.BlockSpec(memory_space=pltpu.VMEM)
HBM = pl.BlockSpec(memory_space=pltpu.HBM)
DAMP = 0.1
STEPS = 5
LEAST = 3e-5


def dot_nt(a, b):
    return lax.dot_general(a, b, (((1,), (1,)), ((), ())), preferred_element_type=jnp.float32)


def dot_hi(a, b):
    return jnp.dot(a, b, precision=HIGH, preferred_element_type=jnp.float32)


def project_kernel(lengths, act, grad, proj_in, proj_out, sketch, live, len_s, act_v, grad_v, pin_v, pout_v, out_v, in_v, sems):
    examples, seq_len, hidden = act.shape
    rank = proj_in.shape[0]
    tokens = examples * seq_len
    stages = sems.shape[0] // 2 - 1
    width = hidden // (stages - 1)
    copies = []

    def begin(src, dst):
        copy = pltpu.make_async_copy(src, dst, sems.at[len(copies)])
        copy.start()
        copies.append(copy)

    begin(proj_out, pout_v)
    begin(grad, grad_v)
    for n in range(stages - 1):
        span = pl.ds(n * width, width)
        begin(proj_in.at[:, span], pin_v.at[:, span])
        begin(act.at[:, :, span], act_v.at[:, :, span])
    begin(lengths, len_s)

    def stage(n):
        copies[2 * n].wait()
        copies[2 * n + 1].wait()
        if n == 0:
            out_v[...] = dot_nt(grad_v[...].reshape(tokens, -1), pout_v[...])
            return
        span = pl.ds((n - 1) * width, width)
        in_part = dot_nt(act_v[:, :, span].reshape(tokens, width), pin_v[:, span])
        if n > 1:
            in_part += in_v[...]
        if n < stages - 1:
            in_v[...] = in_part
            return
        both = jnp.concatenate([out_v[...], in_part], axis=1)
        token = lax.broadcasted_iota(jnp.int32, (seq_len, 2 * rank), 0)
        copies[-1].wait()
        count = jnp.int32(0)
        for e in range(examples):
            rows = pl.ds(e * seq_len, seq_len)
            sketch[rows] = jnp.where(token < len_s[e], both[e * seq_len : (e + 1) * seq_len], 0.0)
            count += len_s[e]
        live[...] = jnp.full(live.shape, count.astype(jnp.float32))

    @pl.loop(0, stages)
    def _(turn):
        for n in range(stages):
            pl.when(turn == n)(functools.partial(stage, n))


def gram_kernel(seq_len, leads, live, mine, theirs, packed):
    rank = mine.shape[1] // 2
    half = rank // 2

    @pl.when(leads())
    def _():
        tokens = mine[...] + theirs[...]
        grams = []
        for e in range(2):
            block = tokens[e * seq_len : (e + 1) * seq_len]
            grams.append(
                lax.dot_general(
                    block, block, (((0,), (0,)), ((), ())), precision=HIGH, preferred_element_type=jnp.float32
                )
            )
        total = grams[0] + grams[1]
        high, low = total[:rank], total[rank:]
        row = lax.broadcasted_iota(jnp.int32, (half, 2 * rank), 0)
        lane = lax.broadcasted_iota(jnp.int32, (half, 2 * rank), 1)
        packed[rank : rank + half] = jnp.where(
            lane < rank,
            jnp.where(lane <= row, high[:half], pltpu.roll(low[:half], rank, 1)),
            jnp.where(lane - rank <= row + half, pltpu.roll(high[half:], rank, 1), low[half:]),
        )
        row = lax.broadcasted_iota(jnp.int32, (rank, 2 * rank), 0)
        lane = lax.broadcasted_iota(jnp.int32, (rank, 2 * rank), 1)
        diag_in = jnp.sum(jnp.where(lane == rank + row, low, 0.0), axis=0, keepdims=True)
        diag_out = jnp.sum(jnp.where(lane == row, high, 0.0), axis=0, keepdims=True)
        tail = jnp.where(row[:8] == 1, live[...], diag_in + diag_out)
        packed[rank + half :] = tail
        packed[:rank] = jnp.where(lane < rank, pltpu.roll(grams[1][:rank], rank, 1), grams[0][:rank])


def merge_kernel(leads, mine, theirs, merged):
    rank = mine.shape[1] // 2

    @pl.when(leads())
    def _():
        merged[:rank] = theirs[:rank]
        merged[rank:] = mine[rank:] + theirs[rank:]


def normalised(rank, total):
    half = rank // 2
    mixed = jnp.concatenate([total[:half, :rank], total[:half, rank:]], axis=0)
    turned = mixed.T
    diag = total[half : half + 1, rank:]
    diags = total[half : half + 1]
    count = total[half + 1 : half + 2, :1]
    row = lax.broadcasted_iota(jnp.int32, (rank, rank), 0)
    lane = lax.broadcasted_iota(jnp.int32, (rank, rank), 1)
    eye = row == lane
    sum_out = jnp.where(lane <= row, mixed, turned)
    sum_in = jnp.where(lane > row, mixed, jnp.where(eye, diag, turned))

    def divide(sums, diag):
        inverse = 1.0 / jnp.sum(diag, axis=1, keepdims=True)
        return sums * inverse + jnp.where(eye, DAMP / rank, 0.0), count * inverse

    return *divide(sum_out, diags[:, :rank]), *divide(sum_in, diags[:, rank:]), jnp.where(eye, 1.0, 0.0)


def total_square(matrix):
    return jnp.sum(jnp.sum(matrix * matrix, axis=0, keepdims=True), axis=1, keepdims=True)


def solve(rank, total, right, held):
    d_out, c_out, d_in, c_in, eye = normalised(rank, total)

    def scale(matrix):
        mean = (1.0 + DAMP) / rank
        spread = jnp.sqrt(jnp.maximum(total_square(matrix) / rank - mean * mean, 0.0))
        return 2.0 / (mean + spread * (rank - 1) ** 0.5 + DAMP / rank)

    s_out, s_in = scale(d_out), scale(d_in)
    t_out = s_out * (2.0 * d_out - s_out * dot_hi(d_out, d_out))
    t_in = s_in * (2.0 * d_in - s_in * dot_hi(d_in, d_in))
    right = 2.0 * right - s_out * dot_hi(d_out, right)
    x_in = 2.0 * eye - s_in * d_in

    def square(t_out, t_in):
        return 2.0 * t_out - dot_hi(t_out, t_out), 2.0 * t_in - dot_hi(t_in, t_in)

    def update(t_out, t_in, right, x_in):
        return 2.0 * right - dot_hi(t_out, right), 2.0 * x_in - dot_hi(x_in, t_in)

    def residual(t_out, t_in):
        return jnp.sum(jnp.maximum(total_square(eye - t_out), total_square(eye - t_in)))

    for n in range(STEPS - 1):
        right, x_in = update(t_out, t_in, right, x_in)
        if n == STEPS - 3:
            early = residual(t_out, t_in)
        if n < STEPS - 2:
            t_out, t_in = square(t_out, t_in)

    for ref, value in zip(held, (t_out, t_in, right, x_in)):
        ref[...] = value

    @pl.when(early * early > 5e-5)
    def _():
        def unfinished(state):
            return jnp.logical_and(state[0] > LEAST, state[1] < 40)

        def more(state):
            _, n, t_out, t_in, right, x_in = state
            t_out, t_in = square(t_out, t_in)
            right, x_in = update(t_out, t_in, right, x_in)
            return residual(t_out, t_in), n + 1, t_out, t_in, right, x_in

        state = (residual(held[0][...], held[1][...]), jnp.int32(0), *[ref[...] for ref in held])
        state = lax.while_loop(unfinished, more, state)
        held[2][...] = state[4]
        held[3][...] = state[5]

    right, x_in = held[2][...], held[3][...]
    return right, x_in, c_out * s_out, c_in * s_in


def finish_kernel(seq_len, leads, masks, count, queries, *refs):
    blocks, scores, held = refs[:-5], refs[-5], refs[-4:]
    rank = blocks[0].shape[1] // 2

    @pl.when(leads())
    def _():
        pairs = [ref[:rank] for ref in blocks]
        total = [ref[rank:] for ref in blocks[:count]]
        while len(total) > 1:
            total = [total[n] + total[n + 1] for n in range(0, len(total), 2)]
        left, inv_in, c_out, c_in = solve(rank, total[0], pairs[masks.index(0)], held)
        left = left * c_out
        zero = jnp.zeros((rank, rank), jnp.float32)
        beside = jnp.concatenate([inv_in, zero, zero, inv_in], axis=1)
        before = jnp.concatenate([zero, inv_in, inv_in, zero], axis=1)
        both = dot_hi(left, jnp.concatenate([beside, before], axis=0)) * c_in
        straight, crossed = both[:, : 2 * rank], both[:, 2 * rank :]
        size = len(pairs)
        sums = [jnp.sum(pair * straight, axis=0, keepdims=True) for pair in pairs]
        sums += [jnp.sum(pair * crossed, axis=0, keepdims=True) for pair in pairs]
        sums = jnp.concatenate(sums, axis=0)
        inner = lax.broadcasted_iota(jnp.int32, sums.shape, 1) < rank
        second = jnp.sum(jnp.where(inner, sums, 0.0), axis=1, keepdims=True)
        first = jnp.sum(jnp.where(inner, 0.0, sums), axis=1, keepdims=True)
        row = lax.broadcasted_iota(jnp.int32, (2 * size, queries.shape[1]), 0)
        mask = sum(jnp.where(row % size == n, value, 0) for n, value in enumerate(masks))
        example = 2 * (lax.axis_index("dp") ^ mask)
        chosen = queries[...]
        scale = 1.0 / (rank * seq_len)
        second = jnp.where(chosen == example + 1, scale * second, 0.0)
        first = jnp.where(chosen == example, scale * first, 0.0)
        same = row < size
        scores[0:1, :] = jnp.sum(jnp.where(same, first, second), axis=0, keepdims=True)
        scores[1:2, :] = jnp.sum(jnp.where(same, second, first), axis=0, keepdims=True)


def publish_kernel(scores, out, sem):
    copy = pltpu.make_async_copy(scores, out, sem)
    copy.start()
    copy.wait()


def replace_kernel(leads, theirs, mine, out, sem):
    @pl.when(jnp.logical_not(leads()))
    def _():
        copy = pltpu.make_async_copy(theirs, out, sem)
        copy.start()
        copy.wait()


def shape(*dims):
    return pltpu.VMEM(dims, jnp.float32)


def call(kernel, name, out_shape, *operands, scratch=()):
    return pl.pallas_call(
        kernel,
        out_shape=out_shape,
        in_specs=[VMEM] * len(operands),
        out_specs=VMEM,
        scratch_shapes=list(scratch),
        compiler_params=pltpu.CompilerParams(vmem_limit_bytes=4 * 2**20),
        name=name,
    )(*[pltpu.with_memory_space_constraint(operand, pltpu.VMEM) for operand in operands])


def project(activations, out_grads, proj_in, proj_out, lengths):
    examples, seq_len, hidden = activations.shape
    rank = proj_in.shape[0]
    stages = 3 if hidden % 256 == 0 else 2
    operands = [lengths, activations, out_grads, proj_in, proj_out]
    return pl.pallas_call(
        project_kernel,
        out_shape=[shape(examples * seq_len, 2 * rank), shape(8, 2 * rank)],
        in_specs=[HBM] * 5,
        out_specs=[VMEM] * 2,
        scratch_shapes=[pltpu.SMEM(lengths.shape, jnp.int32)]
        + [pltpu.VMEM(operand.shape, jnp.bfloat16) for operand in operands[1:]]
        + [pltpu.VMEM((examples * seq_len, rank), jnp.float32)] * 2
        + [pltpu.SemaphoreType.DMA((2 * stages + 2,))],
        compiler_params=pltpu.CompilerParams(vmem_limit_bytes=24 * 2**20),
        name="project",
    )(*[pltpu.with_memory_space_constraint(operand, pltpu.HBM) for operand in operands])


def swap(x, dp, tensor, far, near):
    pairs = []
    for d in range(dp):
        for t in range(tensor):
            masks = far if t % 2 else near
            pairs.append((d * tensor + t, (d ^ masks[0]) * tensor + (t ^ masks[1])))
    return lax.ppermute(x, ("dp", "tensor"), pairs)


def across(x, tensor):
    return lax.ppermute(x, "tensor", [(t, t ^ 1) for t in range(tensor)])


def publish(scores):
    return pl.pallas_call(
        publish_kernel,
        out_shape=jax.ShapeDtypeStruct(scores.shape, scores.dtype),
        in_specs=[VMEM],
        out_specs=HBM,
        scratch_shapes=[pltpu.SemaphoreType.DMA],
        compiler_params=pltpu.CompilerParams(vmem_limit_bytes=2**20),
        cost_estimate=pl.CostEstimate(flops=10**9, bytes_accessed=0, transcendentals=0),
        name="publish",
    )(pltpu.with_memory_space_constraint(scores, pltpu.VMEM))


def replace(theirs, mine, leads):
    return pl.pallas_call(
        functools.partial(replace_kernel, leads),
        out_shape=jax.ShapeDtypeStruct(mine.shape, mine.dtype),
        in_specs=[VMEM, HBM],
        out_specs=HBM,
        scratch_shapes=[pltpu.SemaphoreType.DMA],
        input_output_aliases={1: 0},
        compiler_params=pltpu.CompilerParams(vmem_limit_bytes=2**20),
        name="replace",
    )(pltpu.with_memory_space_constraint(theirs, pltpu.VMEM), mine)


def per_device(dp, tensor, activations, out_grads, proj_in, proj_out, lengths, query_ids):
    examples, seq_len, _ = activations.shape
    rank = proj_in.shape[1]
    num = query_ids.shape[0]
    paired = dp == 4 and tensor == 4
    odd = lambda: lax.rem(lax.axis_index("tensor"), 2) == 1
    leads = odd if paired else lambda: True
    sketch, live = project(activations, out_grads, proj_in.T, proj_out.T, lengths)
    sketch = sketch + across(sketch, tensor)
    if paired:
        other = swap(sketch, dp, tensor, (0, 2), (1, 0))
    else:
        other = jnp.zeros_like(sketch)
        step = 2
        while step < tensor:
            sketch = sketch + lax.ppermute(sketch, "tensor", [(t, t ^ step) for t in range(tensor)])
            step *= 2
    packed = call(
        functools.partial(gram_kernel, seq_len, leads),
        "gram",
        shape(rank + rank // 2 + 8, 2 * rank),
        live,
        sketch,
        other,
    )
    if paired:
        own = packed
        near = swap(packed, dp, tensor, (1, 0), (0, 2))
        other = swap(packed, dp, tensor, (2, 0), (0, 2))
        merged = call(
            functools.partial(merge_kernel, leads), "merge", shape(rank + rank // 2 + 8, 2 * rank), packed, other
        )
        blocks = [merged, swap(merged, dp, tensor, (1, 0), (0, 2)), own, near]
        masks = [2, 3, 0, 1]
        count = 2
    else:
        masks = list(range(dp))
        count = dp
        order = lax.axis_index("dp") ^ jnp.arange(dp, dtype=jnp.int32)
        gathered = lax.all_gather(packed, "dp", axis=0)[order]
        blocks = [gathered[n] for n in range(dp)]
    scores = call(
        functools.partial(finish_kernel, seq_len, leads, masks, count),
        "finish",
        shape(examples, num),
        query_ids.reshape(1, num),
        *blocks,
        scratch=[shape(rank, rank), shape(rank, rank), shape(rank, 2 * rank), shape(rank, rank)],
    )
    if paired:
        other = across(scores, tensor)
        scores = replace(other, publish(scores), leads)
    return scores.T


def solution(mesh):
    placed = (
        P(("groups", "dp"), None, "tensor"),
        P(("groups", "dp"), None, "tensor"),
        P("tensor", None),
        P("tensor", None),
        P(("groups", "dp")),
        P("groups"),
    )
    return jax.shard_map(
        functools.partial(per_device, mesh.shape["dp"], mesh.shape["tensor"]),
        mesh=mesh,
        in_specs=placed,
        out_specs=P(None, ("groups", "dp")),
        check_vma=False,
    )
```

```python
import functools

import jax
import jax.numpy as jnp
from jax import lax
from jax.experimental import pallas as pl
from jax.experimental.pallas import tpu as pltpu
from jax.sharding import PartitionSpec as P

HIGH = lax.Precision.HIGHEST
VMEM = pl.BlockSpec(memory_space=pltpu.VMEM)
HBM = pl.BlockSpec(memory_space=pltpu.HBM)
DAMP = 0.1
STEPS = 5


def dot_nt(a, b):
    return lax.dot_general(a, b, (((1,), (1,)), ((), ())), preferred_element_type=jnp.float32)


def dot_hi(a, b):
    return jnp.dot(a, b, precision=HIGH, preferred_element_type=jnp.float32)


def project_kernel(lengths, act, grad, proj_in, proj_out, sketch, live, len_s, act_v, grad_v, pin_v, pout_v, in_v, sems):
    examples, seq_len, hidden = act.shape
    rank = proj_in.shape[0]
    tokens = examples * seq_len
    stages = sems.shape[0] // 2 - 1
    width = hidden // (stages - 1)
    copies = []

    def begin(src, dst):
        copy = pltpu.make_async_copy(src, dst, sems.at[len(copies)])
        copy.start()
        copies.append(copy)

    begin(lengths, len_s)
    begin(proj_out, pout_v)
    begin(grad, grad_v)
    for n in range(stages - 1):
        span = pl.ds(n * width, width)
        begin(proj_in.at[:, span], pin_v.at[:, span])
        begin(act.at[:, :, span], act_v.at[:, :, span])

    def store(part, lanes):
        token = lax.broadcasted_iota(jnp.int32, (seq_len, rank), 0)
        for e in range(examples):
            rows = slice(e * seq_len, (e + 1) * seq_len)
            sketch[rows, lanes] = jnp.where(token < len_s[e], part[rows], 0.0)

    def stage(n):
        if n == 0:
            copies[0].wait()
            count = sum(len_s[e] for e in range(examples))
            live[...] = jnp.full(live.shape, count.astype(jnp.float32))
        copies[2 * n + 1].wait()
        copies[2 * n + 2].wait()
        if n == 0:
            store(dot_nt(grad_v[...].reshape(tokens, -1), pout_v[...]), slice(0, rank))
            return
        span = pl.ds((n - 1) * width, width)
        in_part = dot_nt(act_v[:, :, span].reshape(tokens, width), pin_v[:, span])
        if n > 1:
            in_part += in_v[...]
        if n < stages - 1:
            in_v[...] = in_part
        else:
            store(in_part, slice(rank, 2 * rank))

    @pl.loop(0, stages)
    def _(turn):
        for n in range(stages):
            pl.when(turn == n)(functools.partial(stage, n))


def gram_kernel(seq_len, leads, live, mine, theirs, packed):
    rank = mine.shape[1] // 2
    half = rank // 2

    @pl.when(leads())
    def _():
        tokens = mine[...] + theirs[...]
        grams = []
        for e in range(2):
            block = tokens[e * seq_len : (e + 1) * seq_len]
            grams.append(
                lax.dot_general(
                    block, block, (((0,), (0,)), ((), ())), precision=HIGH, preferred_element_type=jnp.float32
                )
            )
        total = grams[0] + grams[1]
        high, low = total[:rank], total[rank:]
        row = lax.broadcasted_iota(jnp.int32, (half, 2 * rank), 0)
        lane = lax.broadcasted_iota(jnp.int32, (half, 2 * rank), 1)
        packed[rank : rank + half] = jnp.where(
            lane < rank,
            jnp.where(lane <= row, high[:half], pltpu.roll(low[:half], rank, 1)),
            jnp.where(lane - rank <= row + half, pltpu.roll(high[half:], rank, 1), low[half:]),
        )
        row = lax.broadcasted_iota(jnp.int32, (rank, 2 * rank), 0)
        lane = lax.broadcasted_iota(jnp.int32, (rank, 2 * rank), 1)
        diag_in = jnp.sum(jnp.where(lane == rank + row, low, 0.0), axis=0, keepdims=True)
        diag_out = jnp.sum(jnp.where(lane == row, high, 0.0), axis=0, keepdims=True)
        tail = jnp.where(row[:8] == 1, live[...], diag_in + diag_out)
        packed[rank + half :] = tail
        packed[:rank] = jnp.where(lane < rank, pltpu.roll(grams[1][:rank], rank, 1), grams[0][:rank])


def merge_kernel(leads, mine, theirs, merged):
    rank = mine.shape[1] // 2

    @pl.when(leads())
    def _():
        merged[:rank] = theirs[:rank]
        merged[rank:] = mine[rank:] + theirs[rank:]


def normalised(rank, total):
    half = rank // 2
    mixed = jnp.concatenate([total[:half, :rank], total[:half, rank:]], axis=0)
    turned = mixed.T
    diag = total[half : half + 1, rank:]
    diags = total[half : half + 1]
    count = total[half + 1 : half + 2, :1]
    row = lax.broadcasted_iota(jnp.int32, (rank, rank), 0)
    lane = lax.broadcasted_iota(jnp.int32, (rank, rank), 1)
    eye = row == lane
    sum_out = jnp.where(lane <= row, mixed, turned)
    sum_in = jnp.where(lane > row, mixed, jnp.where(eye, diag, turned))

    def divide(sums, diag):
        inverse = 1.0 / jnp.sum(diag, axis=1, keepdims=True)
        return sums * inverse + jnp.where(eye, DAMP / rank, 0.0), count * inverse

    return *divide(sum_out, diags[:, :rank]), *divide(sum_in, diags[:, rank:]), jnp.where(eye, 1.0, 0.0)


def total_square(matrix):
    return jnp.sum(jnp.sum(matrix * matrix, axis=0, keepdims=True), axis=1, keepdims=True)


def solve(rank, total, right):
    d_out, c_out, d_in, c_in, eye = normalised(rank, total)

    def scale(matrix):
        mean = (1.0 + DAMP) / rank
        spread = jnp.sqrt(jnp.maximum(total_square(matrix) / rank - mean * mean, 0.0))
        return 2.0 / (mean + spread * (rank - 1) ** 0.5 + DAMP / rank)

    s_out, s_in = scale(d_out), scale(d_in)
    t_out = s_out * (2.0 * d_out - s_out * dot_hi(d_out, d_out))
    t_in = s_in * (2.0 * d_in - s_in * dot_hi(d_in, d_in))
    right = 2.0 * right - s_out * dot_hi(d_out, right)
    x_in = 2.0 * eye - s_in * d_in

    def square(t_out, t_in):
        return 2.0 * t_out - dot_hi(t_out, t_out), 2.0 * t_in - dot_hi(t_in, t_in)

    def update(t_out, t_in, right, x_in):
        return 2.0 * right - dot_hi(t_out, right), 2.0 * x_in - dot_hi(x_in, t_in)

    def residual(t_out, t_in):
        return jnp.sum(jnp.maximum(total_square(eye - t_out), total_square(eye - t_in)))

    for n in range(STEPS - 1):
        right, x_in = update(t_out, t_in, right, x_in)
        if n < STEPS - 2:
            t_out, t_in = square(t_out, t_in)

    def unfinished(state):
        return jnp.logical_and(state[0] > 3e-5, state[1] < 40)

    def more(state):
        _, n, t_out, t_in, right, x_in = state
        t_out, t_in = square(t_out, t_in)
        right, x_in = update(t_out, t_in, right, x_in)
        return residual(t_out, t_in), n + 1, t_out, t_in, right, x_in

    state = (residual(t_out, t_in), jnp.int32(0), t_out, t_in, right, x_in)
    _, _, _, _, right, x_in = lax.while_loop(unfinished, more, state)
    return right, x_in, c_out * s_out, c_in * s_in


def finish_kernel(seq_len, leads, masks, count, queries, *refs):
    blocks, scores = refs[:-1], refs[-1]
    rank = blocks[0].shape[1] // 2

    @pl.when(leads())
    def _():
        pairs = [ref[:rank] for ref in blocks]
        total = [ref[rank:] for ref in blocks[:count]]
        while len(total) > 1:
            total = [total[n] + total[n + 1] for n in range(0, len(total), 2)]
        left, inv_in, c_out, c_in = solve(rank, total[0], pairs[masks.index(0)])
        left = left * c_out
        zero = jnp.zeros((rank, rank), jnp.float32)
        beside = jnp.concatenate([inv_in, zero, zero, inv_in], axis=1)
        before = jnp.concatenate([zero, inv_in, inv_in, zero], axis=1)
        both = dot_hi(left, jnp.concatenate([beside, before], axis=0)) * c_in
        straight, crossed = both[:, : 2 * rank], both[:, 2 * rank :]
        size = len(pairs)
        sums = [jnp.sum(pair * straight, axis=0, keepdims=True) for pair in pairs]
        sums += [jnp.sum(pair * crossed, axis=0, keepdims=True) for pair in pairs]
        sums = jnp.concatenate(sums, axis=0)
        inner = lax.broadcasted_iota(jnp.int32, sums.shape, 1) < rank
        second = jnp.sum(jnp.where(inner, sums, 0.0), axis=1, keepdims=True)
        first = jnp.sum(jnp.where(inner, 0.0, sums), axis=1, keepdims=True)
        row = lax.broadcasted_iota(jnp.int32, (2 * size, queries.shape[1]), 0)
        mask = sum(jnp.where(row % size == n, value, 0) for n, value in enumerate(masks))
        example = 2 * (lax.axis_index("dp") ^ mask)
        chosen = queries[...]
        scale = 1.0 / (rank * seq_len)
        second = jnp.where(chosen == example + 1, scale * second, 0.0)
        first = jnp.where(chosen == example, scale * first, 0.0)
        same = row < size
        scores[0:1, :] = jnp.sum(jnp.where(same, first, second), axis=0, keepdims=True)
        scores[1:2, :] = jnp.sum(jnp.where(same, second, first), axis=0, keepdims=True)


def publish_kernel(scores, out, sem):
    copy = pltpu.make_async_copy(scores, out, sem)
    copy.start()
    copy.wait()


def replace_kernel(leads, theirs, mine, out, sem):
    @pl.when(jnp.logical_not(leads()))
    def _():
        copy = pltpu.make_async_copy(theirs, out, sem)
        copy.start()
        copy.wait()


def shape(*dims):
    return pltpu.VMEM(dims, jnp.float32)


def call(kernel, name, out_shape, *operands):
    return pl.pallas_call(
        kernel,
        out_shape=out_shape,
        in_specs=[VMEM] * len(operands),
        out_specs=VMEM,
        compiler_params=pltpu.CompilerParams(vmem_limit_bytes=4 * 2**20),
        name=name,
    )(*[pltpu.with_memory_space_constraint(operand, pltpu.VMEM) for operand in operands])


def project(activations, out_grads, proj_in, proj_out, lengths):
    examples, seq_len, hidden = activations.shape
    rank = proj_in.shape[0]
    stages = 3 if hidden % 256 == 0 else 2
    operands = [lengths, activations, out_grads, proj_in, proj_out]
    return pl.pallas_call(
        project_kernel,
        out_shape=[shape(examples * seq_len, 2 * rank), shape(8, 2 * rank)],
        in_specs=[HBM] * 5,
        out_specs=[VMEM] * 2,
        scratch_shapes=[pltpu.SMEM(lengths.shape, jnp.int32)]
        + [pltpu.VMEM(operand.shape, jnp.bfloat16) for operand in operands[1:]]
        + [pltpu.VMEM((examples * seq_len, rank), jnp.float32)]
        + [pltpu.SemaphoreType.DMA((2 * stages + 2,))],
        compiler_params=pltpu.CompilerParams(vmem_limit_bytes=24 * 2**20),
        name="project",
    )(*[pltpu.with_memory_space_constraint(operand, pltpu.HBM) for operand in operands])


def swap(x, dp, tensor, far, near):
    pairs = []
    for d in range(dp):
        for t in range(tensor):
            masks = far if t % 2 else near
            pairs.append((d * tensor + t, (d ^ masks[0]) * tensor + (t ^ masks[1])))
    return lax.ppermute(x, ("dp", "tensor"), pairs)


def across(x, tensor):
    return lax.ppermute(x, "tensor", [(t, t ^ 1) for t in range(tensor)])


def publish(scores):
    return pl.pallas_call(
        publish_kernel,
        out_shape=jax.ShapeDtypeStruct(scores.shape, scores.dtype),
        in_specs=[VMEM],
        out_specs=HBM,
        scratch_shapes=[pltpu.SemaphoreType.DMA],
        compiler_params=pltpu.CompilerParams(vmem_limit_bytes=2**20),
        cost_estimate=pl.CostEstimate(flops=10**9, bytes_accessed=0, transcendentals=0),
        name="publish",
    )(pltpu.with_memory_space_constraint(scores, pltpu.VMEM))


def replace(theirs, mine, leads):
    return pl.pallas_call(
        functools.partial(replace_kernel, leads),
        out_shape=jax.ShapeDtypeStruct(mine.shape, mine.dtype),
        in_specs=[VMEM, HBM],
        out_specs=HBM,
        scratch_shapes=[pltpu.SemaphoreType.DMA],
        input_output_aliases={1: 0},
        compiler_params=pltpu.CompilerParams(vmem_limit_bytes=2**20),
        name="replace",
    )(pltpu.with_memory_space_constraint(theirs, pltpu.VMEM), mine)


def per_device(dp, tensor, activations, out_grads, proj_in, proj_out, lengths, query_ids):
    examples, seq_len, _ = activations.shape
    rank = proj_in.shape[1]
    num = query_ids.shape[0]
    paired = dp == 4 and tensor == 4
    odd = lambda: lax.rem(lax.axis_index("tensor"), 2) == 1
    leads = odd if paired else lambda: True
    sketch, live = project(activations, out_grads, proj_in.T, proj_out.T, lengths)
    sketch = sketch + across(sketch, tensor)
    if paired:
        other = swap(sketch, dp, tensor, (0, 2), (1, 0))
    else:
        other = jnp.zeros_like(sketch)
        step = 2
        while step < tensor:
            sketch = sketch + lax.ppermute(sketch, "tensor", [(t, t ^ step) for t in range(tensor)])
            step *= 2
    packed = call(
        functools.partial(gram_kernel, seq_len, leads),
        "gram",
        shape(rank + rank // 2 + 8, 2 * rank),
        live,
        sketch,
        other,
    )
    if paired:
        own = packed
        near = swap(packed, dp, tensor, (1, 0), (0, 2))
        other = swap(packed, dp, tensor, (2, 0), (0, 2))
        merged = call(
            functools.partial(merge_kernel, leads), "merge", shape(rank + rank // 2 + 8, 2 * rank), packed, other
        )
        blocks = [merged, swap(merged, dp, tensor, (1, 0), (0, 2)), own, near]
        masks = [2, 3, 0, 1]
        count = 2
    else:
        masks = list(range(dp))
        count = dp
        order = lax.axis_index("dp") ^ jnp.arange(dp, dtype=jnp.int32)
        gathered = lax.all_gather(packed, "dp", axis=0)[order]
        blocks = [gathered[n] for n in range(dp)]
    scores = call(
        functools.partial(finish_kernel, seq_len, leads, masks, count),
        "finish",
        shape(examples, num),
        query_ids.reshape(1, num),
        *blocks,
    )
    if paired:
        other = across(scores, tensor)
        scores = replace(other, publish(scores), leads)
    return scores.T


def solution(mesh):
    placed = (
        P(("groups", "dp"), None, "tensor"),
        P(("groups", "dp"), None, "tensor"),
        P("tensor", None),
        P("tensor", None),
        P(("groups", "dp")),
        P("groups"),
    )
    return jax.shard_map(
        functools.partial(per_device, mesh.shape["dp"], mesh.shape["tensor"]),
        mesh=mesh,
        in_specs=placed,
        out_specs=P(None, ("groups", "dp")),
        check_vma=False,
    )
```
